256 devices in a mesh: dp: 32 (over z, x_hi, core), weight: 8 (over y, x_lo).
Axes of the slice: x: 4 (x_hi: 2, x_lo: 2; x = x_hi * 2 + x_lo), y: 4, z: 8, core: 2. Of those that a mesh axis runs over, the one named last changes fastest.
Arguments:
- tokens: bfloat16 [1024, 4096], P('weight'), may hold values from -6 to 6
- cotangent: bfloat16 [1024, 4096], P('weight'), may hold values from -6 to 6
- step_lengths: int32 [8, 4], P('weight'), may hold values from 1 to 64, 128 in all within a row
- step_labels: int32 [8, 4], P('weight'), may hold values from 0 to 1
- gate_weight: bfloat16 [16384, 4096], P(('dp', 'weight')), may hold values from -0.09375 to 0.09375
- up_weight: bfloat16 [16384, 4096], P(('dp', 'weight')), may hold values from -0.09375 to 0.09375
- down_weight: bfloat16 [16384, 4096], P(('dp', 'weight')), may hold values from -0.046875 to 0.046875
Outputs:
- input_grad: bfloat16 [1024, 4096], P('weight', 'dp')
- gate_grad: float32 [16384, 4096], P(('dp', 'weight'))
- up_grad: float32 [16384, 4096], P(('dp', 'weight'))
- down_grad: float32 [16384, 4096], P(('dp', 'weight'))
The draws below stay inside these ranges and needn't reach their ends.
All inputs are finite; a program needn't handle non-finite values.
Results may differ from the reference program's by a relative error of at most 0.0057.
Values may be sent and summed in bfloat16 or wider, within the bound.
A program may use at most 128 MiB of HBM per device.

```python
import math
import jax
import jax.numpy as jnp
import numpy as np
from jax import lax

D = 4096
FF = 16384
STEPS = 4
TRACE = 128
TRACES = 8
TOKENS = 1024


def place_ends(drawn, stream_key, low, top_value):
    dims = drawn.shape
    index_at = [jax.random.randint(jax.random.fold_in(stream_key, axis), (), 0, dims[axis]) for axis in range(len(dims))]
    drawn = drawn.at[tuple(index_at)].set(low)
    longest = dims.index(max(dims))
    index_at[longest] = (index_at[longest] + 1) % dims[longest]
    return drawn.at[tuple(index_at)].set(top_value)


def level_of(own_key, shape, cuts, least, high):
    def one(dim, blocks):
        draws = jax.random.uniform(jax.random.fold_in(jax.random.fold_in(own_key, 6), dim), (blocks,), jnp.float32, least / len(cuts), high / len(cuts))
        return jnp.repeat(jnp.exp(draws), shape[dim] // blocks).reshape((-1,) + (1,) * (len(shape) - dim - 1))

    factor_of = one(*cuts[0])
    for cut in cuts[1:]:
        factor_of = factor_of * one(*cut)
    return factor_of


def split_up(amount, total, bound, skew):
    portions = [(1 << 20) // math.isqrt(rank ** skew) + 1 for rank in range(2, amount + 1)]
    surplus, holding = total - bound - (amount - 1), [1] * (amount - 1)
    while surplus > 0:
        free = [i for i in range(amount - 1) if holding[i] < bound]
        whole, remaining = sum([portions[i] for i in free]), surplus
        for i in free:
            addition = min(bound - holding[i], max(1, remaining * portions[i] // whole), surplus)
            holding[i] = holding[i] + addition
            surplus = surplus - addition
    return np.array([bound] + holding)


def ragged(rng, count, total, reach, slope):
    if count == 2:
        one = jax.random.randint(rng, (), max(1, total - reach), min(reach, total - 1) + 1)
        return jnp.stack([one, total - one])
    tallies = jnp.asarray(split_up(count, total, reach, slope), jnp.int32)
    couples = (count - 1) // 2
    donor, sink = tallies[1:1 + 2 * couples:2], tallies[2:2 + 2 * couples:2]
    slack = jnp.minimum(donor - 1, reach - sink)
    passed = jax.random.randint(jax.random.fold_in(rng, 1), (couples,), 0, 1 << 20) % (slack + 1)
    tallies = tallies.at[1:1 + 2 * couples:2].set(donor - passed).at[2:2 + 2 * couples:2].set(sink + passed)
    return tallies[jax.random.permutation(jax.random.fold_in(rng, 2), count)]


def centred(stream_key, extent, spread, bound, shards=(), held_as=jnp.bfloat16):
    array = jax.random.normal(stream_key, extent, jnp.float32) * spread
    if len(shards) > 0:
        array = level_of(stream_key, extent, shards, -0.22, 0.18) * array
    return jnp.clip(array, min=-bound, max=bound).astype(held_as)


def setup_inputs(seed: int = 0) -> dict:
    streams_of = jax.random.split(jax.random.key(seed), 8)
    tokens = centred(streams_of[0], (TOKENS, D), 1.0, 6.0, ((0, 8),))
    cotangent = centred(streams_of[1], (TOKENS, D), 1.0, 6.0, ((0, 8),))
    step_lengths = jax.vmap(lambda own: ragged(own, STEPS, TRACE, TRACE // 2, 1))(jax.random.split(streams_of[2], TRACES)).reshape((TRACES, STEPS)).astype(jnp.int32)
    step_labels = place_ends(jax.random.randint(streams_of[3], (TRACES, STEPS), 0, 2), jax.random.fold_in(streams_of[3], 1), 0, 1).astype(jnp.int32)
    gate_weight = centred(streams_of[4], (FF, D), D ** -0.5, 0.09375, ((0, 256),))
    up_weight = centred(streams_of[5], (FF, D), D ** -0.5, 0.09375, ((0, 256),))
    down_weight = centred(streams_of[6], (FF, D), FF ** -0.5, 0.046875, ((0, 256),))
    return {"tokens": tokens, "cotangent": cotangent, "step_lengths": step_lengths, "step_labels": step_labels, "gate_weight": gate_weight, "up_weight": up_weight, "down_weight": down_weight}


def contract_rows(left, right):
    return lax.dot_general(left, right, (((0,), (0,)), ((), ())), preferred_element_type=jnp.float32)

def contract_cols(left, right):
    return lax.dot_general(left, right, (((1,), (1,)), ((), ())), preferred_element_type=jnp.float32)

def reference(tokens, cotangent, step_lengths, step_labels, gate_weight, up_weight, down_weight):
    ends = jnp.cumsum(step_lengths, axis=1).astype(jnp.int32)
    position = jnp.arange(TRACE, dtype=jnp.int32)
    segment = lax.optimization_barrier(jnp.sum((position[None, :, None] >= ends[:, None, :]).astype(jnp.int32), axis=2))
    onehot = (segment[:, :, None] == jnp.arange(STEPS, dtype=jnp.int32)[None, None, :]).astype(jnp.float32)
    per_step = (1.0 + 2.0 * step_labels.astype(jnp.float32)) * lax.rsqrt(step_lengths.astype(jnp.float32) * STEPS / TRACE)
    factor = lax.optimization_barrier(jnp.sum(onehot * per_step[:, None, :], axis=2)).reshape(TOKENS)
    weighted = (cotangent.astype(jnp.float32) * factor[:, None]).astype(jnp.bfloat16)
    gate = contract_cols(tokens, gate_weight)
    up = contract_cols(tokens, up_weight)
    sig = jax.nn.sigmoid(gate)
    act = gate * sig
    hidden = (act * up).astype(jnp.bfloat16)
    hidden_grad = contract_cols(weighted, down_weight)
    gate_term = (hidden_grad * up * sig * (1.0 + gate * (1.0 - sig))).astype(jnp.bfloat16)
    up_term = (hidden_grad * act).astype(jnp.bfloat16)
    input_grad = jnp.dot(gate_term, gate_weight, preferred_element_type=jnp.float32) + jnp.dot(up_term, up_weight, preferred_element_type=jnp.float32)
    scale = 1.0 / TOKENS ** 0.5
    gate_grad = contract_rows(gate_term, tokens) * scale
    up_grad = contract_rows(up_term, tokens) * scale
    down_grad = contract_rows(hidden, weighted) * scale
    return (input_grad.astype(jnp.bfloat16), gate_grad, up_grad, down_grad)
```

```python
import jax
import jax.numpy as jnp
from jax import lax
from jax.experimental import pallas as pl
from jax.experimental.pallas import tpu as pltpu
from jax.sharding import PartitionSpec as P

MESH = pl.DeviceIdType.MESH
BF = jnp.bfloat16
F32 = jnp.float32
D = 4096
ROWS = 128
KC = 512
NC = 512


def nt(left, right):
    return lax.dot_general(left, right, (((1,), (1,)), ((), ())), preferred_element_type=F32)


def nn(left, right):
    return jnp.dot(left, right, preferred_element_type=F32)


def kernel(
    lens, labs, tok, cot, wg, wu, wd,
    o_dx, o_g, o_u, o_d,
    X, C, CT, W, ACC, TERMS, TT, SEND, OWNZ, RECV, ZSEND, ZRECV, DW,
    PART, R1A, R1B, QA, QB, R2A, R2B, F, R3, OUT,
    in_sem, ysend, yrecv, xsend, xrecv, zsend, zrecv, dsend, drecv,
    gsend, grecv, zgsend, zgrecv, s1send, s1recv, s2send, s2recv, s3send, s3recv, out_sem,
):
    dp = lax.axis_index("dp")
    wt = lax.axis_index("weight")
    z, xh, c = dp // 4, (dp // 2) % 2, dp % 2
    y, xl = wt // 2, wt % 2
    x = xh * 2 + xl

    def at(dx=0, dy=0, dz=0, dc=0):
        xx = (x + dx) % 4
        yy = (y + dy) % 4
        zz = (z + dz) % 8
        cc = (c + dc) % 2
        return (zz * 4 + (xx // 2) * 2 + cc, yy * 2 + xx % 2)

    def remote(src, dst, ssem, rsem, where):
        return pltpu.make_async_remote_copy(
            src_ref=src, dst_ref=dst, send_sem=ssem, recv_sem=rsem,
            device_id=where, device_id_type=MESH,
        )

    barrier = pltpu.get_barrier_semaphore()
    partners = [at(dz=dz, dc=dc) for dz in range(8) for dc in range(2) if dz or dc]
    partners += [at(dy=d) for d in (1, 2, 3)] + [at(dx=d) for d in (1, 2, 3)]
    for who in partners:
        pl.semaphore_signal(barrier, inc=1, device_id=who, device_id_type=MESH)

    row0 = pl.multiple_of((z % 2) * 64 + c * 32, 32)
    loads = [pltpu.make_async_copy(cot.at[pl.ds(row0, 32)], CT, in_sem.at[0])]
    for p in range(2):
        loads.append(pltpu.make_async_copy(tok.at[pl.ds(row0 + 16 * p, 16)], X.at[0, p], in_sem.at[1 + p]))
    for m, ref in enumerate((wg, wu, wd)):
        loads.append(pltpu.make_async_copy(ref, W.at[m, pl.ds(192, 64)], in_sem.at[3 + m]))
    for copy in loads:
        copy.start()

    position = lax.broadcasted_iota(jnp.int32, (32, 128), 0) + row0
    segment = jnp.zeros((32, 128), jnp.int32)
    end = lens[0, 0]
    segment = segment + (position >= end).astype(jnp.int32)
    for k in range(1, 4):
        end = end + lens[0, k]
        segment = segment + (position >= end).astype(jnp.int32)
    length = jnp.zeros((32, 128), jnp.int32)
    label = jnp.zeros((32, 128), jnp.int32)
    for k in range(4):
        length = jnp.where(segment == k, lens[0, k], length)
        label = jnp.where(segment == k, labs[0, k], label)
    factor = (1.0 + 2.0 * label.astype(F32)) * lax.rsqrt(length.astype(F32) * 4 / ROWS)
    loads[0].wait()
    for j in range(D // 128):
        cols = slice(j * 128, (j + 1) * 128)
        value = (CT[:, cols].astype(F32) * factor).astype(BF)
        C[0, 0, :, cols] = value[:16]
        C[0, 1, :, cols] = value[16:]
    for copy in loads[1:]:
        copy.wait()
    pl.semaphore_wait(barrier, len(partners))

    sends = []

    def go(copy):
        copy.start()
        sends.append(copy)
        return copy

    arrays = (X, C)

    def y_piece(a, p, way, hop):
        dy_src = 0 if hop == 0 else (4 - way) % 4
        dy_dst = (dy_src - way) % 4
        k = (0 if way == 1 else 1) * 6 + (a * 2 + p if hop == 0 else 4 + a)
        return remote(
            arrays[a].at[dy_src * 2, p], arrays[a].at[dy_dst * 2, p],
            ysend.at[k], yrecv.at[k], at(dy=way),
        )

    def x_piece(a, p, dy):
        way = 1 if p == 0 else -1
        k = p * 8 + dy * 2 + a
        return remote(
            arrays[a].at[dy * 2, p], arrays[a].at[dy * 2 + 1, p],
            xsend.at[k], xrecv.at[k], at(dx=way),
        )

    def z_weights(m, way):
        src = 192 if way == 1 else 224
        dst = 64 if way == 1 else 96
        k = m * 2 + (0 if way == 1 else 1)
        return remote(
            W.at[m, pl.ds(src, 32)], W.at[m, pl.ds(dst, 32)],
            zsend.at[k], zrecv.at[k], at(dz=way),
        )

    def d_own(m):
        return remote(
            W.at[m, pl.ds(192, 64)], W.at[m, pl.ds(128, 64)],
            dsend.at[m], drecv.at[m], at(dc=1),
        )

    def d_forward(m, way):
        src = 64 if way == 1 else 96
        dst = 0 if way == 1 else 32
        k = 3 + m * 2 + (0 if way == 1 else 1)
        return remote(
            W.at[m, pl.ds(src, 32)], W.at[m, pl.ds(dst, 32)],
            dsend.at[k], drecv.at[k], at(dc=1),
        )

    for a in range(2):
        for i in range(2):
            for way in (1, -1):
                go(y_piece(a, i if way == 1 else 1 - i, way, 0))
            if i == 0:
                go(x_piece(a, 0, 0))
                go(x_piece(a, 1, 0))
        if a == 0:
            for m in range(3):
                for way in (1, -1):
                    go(z_weights(m, way))
    for m in range(3):
        go(d_own(m))

    for a in range(2):
        for i in range(2):
            for way in (1, -1):
                p = i if way == 1 else 1 - i
                y_piece(a, p, way, 0).wait_recv()
                if i == 0:
                    go(y_piece(a, p, way, 1))
                go(x_piece(a, p, 3 if way == 1 else 1))
    for m in range(3):
        for way in (1, -1):
            z_weights(m, way).wait_recv()
            go(d_forward(m, way))
    for a in range(2):
        for way in (1, -1):
            p = 0 if way == 1 else 1
            y_piece(a, p, way, 1).wait_recv()
            go(x_piece(a, p, 2))
    for m in range(3):
        d_own(m).wait_recv()
        for way in (1, -1):
            d_forward(m, way).wait_recv()
    for dy in (0, 3, 1, 2):
        for a in range(2):
            for p in range(2):
                x_piece(a, p, dy).wait_recv()

    ACC[...] = jnp.zeros_like(ACC)

    def step(k, carry):
        cols = pl.ds(pl.multiple_of(k * KC, KC), KC)
        left = X[:, :, :, cols].reshape(256, KC)
        ACC[0] += nt(left, W[0, :, cols])
        ACC[1] += nt(left, W[1, :, cols])
        left = C[:, :, :, cols].reshape(256, KC)
        ACC[2] += nt(left, W[2, :, cols])
        return carry

    lax.fori_loop(0, D // KC, step, 0)
    gate, up, hidden_grad = ACC[0], ACC[1], ACC[2]
    sig = jax.nn.sigmoid(gate)
    act = gate * sig
    hidden = act * up
    gate_term = hidden_grad * up * sig * (1.0 + gate * (1.0 - sig))
    up_term = hidden_grad * act
    TERMS[:, :256] = gate_term.astype(BF)
    TERMS[:, 256:] = up_term.astype(BF)
    TT[0] = gate_term.T.astype(BF)
    TT[1] = up_term.T.astype(BF)
    TT[2] = hidden.T.astype(BF)

    def weight_grads(first, m, cols):
        right = (C if m == 2 else X)[:, :, :, cols].reshape(256, NC)
        return nn(TT[m, pl.ds(first, 128)], right)

    def grad_to_sibling(half, m):
        k = half * 3 + m
        return remote(SEND.at[half, m], RECV.at[half, m], gsend.at[k], grecv.at[k], at(dc=1))

    def grads(half, keep):
        for m in range(3):
            def tile(j, carry):
                cols = pl.ds(pl.multiple_of(j * NC, NC), NC)
                value = weight_grads(half * 128, m, cols)
                SEND[half, m, :, cols] = value[:64].astype(BF)
                keep[m, :, cols] = value[64:]
                return carry

            lax.fori_loop(0, D // NC, tile, 0)
            go(grad_to_sibling(half, m))

    grads(0, OWNZ)

    def dx_tile(k, carry):
        cols = pl.ds(pl.multiple_of(k * 256, 256), 256)
        value = nn(TERMS[:, :256], W[0, :, cols]) + nn(TERMS[:, 256:], W[1, :, cols])
        PART[k // 2, k % 2] = value.astype(BF).reshape(4, 2, 32, 256)
        return carry

    def x_hi(dx):
        return ((x + dx) % 4) // 2

    def s1a(dy):
        return remote(PART.at[pl.ds(0, 4), :, dy], R1A.at[dy - 1], s1send.at[dy - 1], s1recv.at[dy - 1], at(dy=dy))

    def s1b(dx):
        return remote(
            PART.at[pl.ds(4, 4), x_hi(dx), :, dx % 2], R1B.at[dx - 1],
            s1send.at[2 + dx], s1recv.at[2 + dx], at(dx=dx),
        )

    def s2a(dx):
        return remote(QA.at[:, x_hi(dx), dx % 2], R2A.at[dx - 1], s2send.at[dx - 1], s2recv.at[dx - 1], at(dx=dx))

    def s2b(dy):
        return remote(QB.at[:, dy], R2B.at[dy - 1], s2send.at[2 + dy], s2recv.at[2 + dy], at(dy=dy))

    def s3(dz, dc):
        k = dz * 2 + dc
        return remote(
            F.at[(z + dz) % 8, (c + dc) % 2], R3.at[k], s3send.at[k], s3recv.at[k], at(dz=dz, dc=dc),
        )

    lax.fori_loop(0, 8, dx_tile, 0)
    for dy in (2, 1, 3):
        go(s1a(dy))
    lax.fori_loop(8, 16, dx_tile, 0)
    for dx in (2, 1, 3):
        go(s1b(dx))

    def grad_over_z(m, way):
        rows = pl.ds(0 if way == -1 else 32, 32)
        k = m * 2 + (0 if way == -1 else 1)
        return remote(ZSEND.at[m, rows], ZRECV.at[m, rows], zgsend.at[k], zgrecv.at[k], at(dz=way))

    for m in range(3):
        grad_to_sibling(0, m).wait_recv()
        ZSEND[m] = (OWNZ[m] + RECV[0, m].astype(F32)).astype(BF)
        for way in (1, -1):
            go(grad_over_z(m, way))

    grads(1, DW)

    for dy in (1, 3, 2):
        s1a(dy).wait_recv()
    total = PART[0:4, :, 0].astype(F32)
    for i in range(3):
        total = total + R1A[i].astype(F32)
    QA[...] = total.astype(BF)
    for dx in (2, 1, 3):
        go(s2a(dx))
    for dx in (1, 3, 2):
        s1b(dx).wait_recv()
    total = PART[pl.ds(4, 4), xh, :, 0].astype(F32)
    for i in range(3):
        total = total + R1B[i].astype(F32)
    QB[...] = total.astype(BF)
    for dy in (2, 1, 3):
        go(s2b(dy))

    for m in range(3):
        grad_to_sibling(1, m).wait_recv()
        DW[m] = DW[m] + RECV[1, m].astype(F32)

    for dx in (1, 3, 2):
        s2a(dx).wait_recv()
    total = QA[:, xh, 0].astype(F32)
    for i in range(3):
        total = total + R2A[i].astype(F32)
    F[0:4, 0] = total[:, :, :128].astype(BF)
    F[0:4, 1] = total[:, :, 128:].astype(BF)
    for dy in (1, 3, 2):
        s2b(dy).wait_recv()
    total = QB[:, 0].astype(F32)
    for i in range(3):
        total = total + R2B[i].astype(F32)
    F[4:8, 0] = total[:, :, :128].astype(BF)
    F[4:8, 1] = total[:, :, 128:].astype(BF)
    for dz in (4, 3, 5, 2, 6, 1, 7, 0):
        for dc in range(2):
            if dz or dc:
                go(s3(dz, dc))

    outs = []
    for m, ref in enumerate((o_g, o_u, o_d)):
        for way in (1, -1):
            grad_over_z(m, way).wait_recv()
        DW[m] = (DW[m] + ZRECV[m].astype(F32)) * (1.0 / 32.0)
        copy = pltpu.make_async_copy(DW.at[m], ref, out_sem.at[m])
        copy.start()
        outs.append(copy)

    for dz in range(8):
        for dc in range(2):
            if dz or dc:
                s3(dz, dc).wait_recv()
    for odd in range(2):
        for dc in range(2):
            total = None
            for dz in range(odd, 8, 2):
                if dz == 0 and dc == 0:
                    term = F[z, c].astype(F32)
                else:
                    term = R3[dz * 2 + dc].astype(F32)
                total = term if total is None else total + term
            row = pl.multiple_of(((z + odd) % 2) * 64 + ((c + dc) % 2) * 32, 32)
            OUT[pl.ds(row, 32), :] = total.astype(BF)
    copy = pltpu.make_async_copy(OUT, o_dx, out_sem.at[3])
    copy.start()
    outs.append(copy)
    for copy in outs:
        copy.wait()
    for copy in sends:
        copy.wait_send()


def body(tokens, cotangent, step_lengths, step_labels, gate_weight, up_weight, down_weight):
    dma = pltpu.SemaphoreType.DMA
    any_ = pl.BlockSpec(memory_space=pl.ANY)
    smem = pl.BlockSpec(memory_space=pltpu.SMEM)
    grad = jax.ShapeDtypeStruct((64, D), F32)
    return pl.pallas_call(
        kernel,
        name="ffn_backward",
        out_shape=(jax.ShapeDtypeStruct((128, 128), BF), grad, grad, grad),
        in_specs=[smem, smem] + [any_] * 5,
        out_specs=[any_] * 4,
        scratch_shapes=[
            pltpu.VMEM((8, 2, 16, D), BF),
            pltpu.VMEM((8, 2, 16, D), BF),
            pltpu.VMEM((32, D), BF),
            pltpu.VMEM((3, 256, D), BF),
            pltpu.VMEM((3, 256, 256), F32),
            pltpu.VMEM((256, 512), BF),
            pltpu.VMEM((3, 256, 256), BF),
            pltpu.VMEM((2, 3, 64, D), BF),
            pltpu.VMEM((3, 64, D), F32),
            pltpu.VMEM((2, 3, 64, D), BF),
            pltpu.VMEM((3, 64, D), BF),
            pltpu.VMEM((3, 64, D), BF),
            pltpu.VMEM((3, 64, D), F32),
            pltpu.VMEM((8, 2, 4, 2, 32, 256), BF),
            pltpu.VMEM((3, 4, 2, 2, 32, 256), BF),
            pltpu.VMEM((3, 4, 4, 32, 256), BF),
            pltpu.VMEM((4, 2, 2, 32, 256), BF),
            pltpu.VMEM((4, 4, 32, 256), BF),
            pltpu.VMEM((3, 4, 32, 256), BF),
            pltpu.VMEM((3, 4, 32, 256), BF),
            pltpu.VMEM((8, 2, 32, 128), BF),
            pltpu.VMEM((16, 32, 128), BF),
            pltpu.VMEM((128, 128), BF),
            dma((6,)), dma((12,)), dma((12,)), dma((16,)), dma((16,)),
            dma((6,)), dma((6,)), dma((9,)), dma((9,)),
            dma((6,)), dma((6,)), dma((6,)), dma((6,)),
            dma((6,)), dma((6,)), dma((6,)), dma((6,)), dma((16,)), dma((16,)),
            dma((4,)),
        ],
        compiler_params=pltpu.CompilerParams(
            collective_id=0, has_side_effects=True, vmem_limit_bytes=56 * 2**20
        ),
        cost_estimate=pl.CostEstimate(flops=4_300_000_000, bytes_accessed=8_000_000, transcendentals=65536),
    )(step_lengths, step_labels, tokens, cotangent, gate_weight, up_weight, down_weight)


def solution(mesh):
    return jax.shard_map(
        body,
        mesh=mesh,
        in_specs=(
            P("weight", None),
            P("weight", None),
            P("weight", None),
            P("weight", None),
            P(("dp", "weight"), None),
            P(("dp", "weight"), None),
            P(("dp", "weight"), None),
        ),
        out_specs=(
            P("weight", "dp"),
            P(("dp", "weight"), None),
            P(("dp", "weight"), None),
            P(("dp", "weight"), None),
        ),
        check_vma=False,
    )
```

```python
import jax
import jax.numpy as jnp
from jax import lax
from jax.experimental import pallas as pl
from jax.experimental.pallas import tpu as pltpu
from jax.sharding import PartitionSpec as P

MESH = pl.DeviceIdType.MESH
BF = jnp.bfloat16
F32 = jnp.float32
D = 4096
ROWS = 128
KC = 512
NC = 512


def nt(left, right):
    return lax.dot_general(left, right, (((1,), (1,)), ((), ())), preferred_element_type=F32)


def nn(left, right):
    return jnp.dot(left, right, preferred_element_type=F32)


def kernel(
    lens, labs, tok, cot, wg, wu, wd,
    o_dx, o_g, o_u, o_d,
    X, C, CT, W, ACC, TERMS, TT, SEND, OWNZ, RECV, ZSEND, ZRECV,
    PART, TA, TB, RA, RB, QA, QB, R2A, R2B, F, R3,
    in_sem, ysend, yrecv, xsend, xrecv, zsend, zrecv, dsend, drecv,
    gsend, grecv, zgsend, zgrecv, s1send, s1recv, s2send, s2recv, s3send, s3recv,
):
    dp = lax.axis_index("dp")
    wt = lax.axis_index("weight")
    z, xh, c = dp // 4, (dp // 2) % 2, dp % 2
    y, xl = wt // 2, wt % 2
    x = xh * 2 + xl

    def at(dx=0, dy=0, dz=0, dc=0):
        xx = (x + dx) % 4
        yy = (y + dy) % 4
        zz = (z + dz) % 8
        cc = (c + dc) % 2
        return (zz * 4 + (xx // 2) * 2 + cc, yy * 2 + xx % 2)

    def remote(src, dst, ssem, rsem, k, where):
        return pltpu.make_async_remote_copy(
            src_ref=src, dst_ref=dst, send_sem=ssem.at[k], recv_sem=rsem.at[k],
            device_id=where, device_id_type=MESH,
        )

    sends = []

    def go(copy):
        copy.start()
        sends.append(copy)
        return copy

    barrier = pltpu.get_barrier_semaphore()
    partners = [at(dz=dz, dc=dc) for dz in range(8) for dc in range(2) if dz or dc]
    partners += [at(dy=d) for d in (1, 2, 3)] + [at(dx=d) for d in (1, 2, 3)]
    for who in partners:
        pl.semaphore_signal(barrier, inc=1, device_id=who, device_id_type=MESH)

    row0 = pl.multiple_of((z % 2) * 64 + c * 32, 32)
    loads = [pltpu.make_async_copy(cot.at[pl.ds(row0, 32)], CT, in_sem.at[0])]
    for p in range(2):
        loads.append(pltpu.make_async_copy(tok.at[pl.ds(row0 + 16 * p, 16)], X.at[0, p], in_sem.at[1 + p]))
    for m, ref in enumerate((wg, wu, wd)):
        loads.append(pltpu.make_async_copy(ref, W.at[m, pl.ds(192, 64)], in_sem.at[3 + m]))
    for copy in loads:
        copy.start()

    position = lax.broadcasted_iota(jnp.int32, (32, 128), 0) + row0
    segment = jnp.zeros((32, 128), jnp.int32)
    end = lens[0, 0]
    segment = segment + (position >= end).astype(jnp.int32)
    for k in range(1, 4):
        end = end + lens[0, k]
        segment = segment + (position >= end).astype(jnp.int32)
    length = jnp.zeros((32, 128), jnp.int32)
    label = jnp.zeros((32, 128), jnp.int32)
    for k in range(4):
        length = jnp.where(segment == k, lens[0, k], length)
        label = jnp.where(segment == k, labs[0, k], label)
    factor = (1.0 + 2.0 * label.astype(F32)) * lax.rsqrt(length.astype(F32) * 4 / ROWS)
    loads[0].wait()
    for j in range(D // 128):
        cols = slice(j * 128, (j + 1) * 128)
        value = (CT[:, cols].astype(F32) * factor).astype(BF)
        C[0, 0, :, cols] = value[:16]
        C[0, 1, :, cols] = value[16:]
    for copy in loads[1:]:
        copy.wait()
    pl.semaphore_wait(barrier, len(partners))

    arrays = (X, C)

    def first(way):
        return 0 if way == 1 else 1

    def side(way):
        return 3 if way == 1 else 1

    def y_piece(a, p, way):
        k = first(way) * 8 + a * 2 + p
        return remote(arrays[a].at[0, p], arrays[a].at[side(way) * 2, p], ysend, yrecv, k, at(dy=way))

    def y_next(a, way):
        p = first(way)
        k = first(way) * 8 + 4 + a
        return remote(arrays[a].at[side(way) * 2, p], arrays[a].at[4, p], ysend, yrecv, k, at(dy=way))

    def y_other(way):
        p = first(way)
        k = first(way) * 8 + 6
        return remote(C.at[side(way) * 2 + 1, p], C.at[5, p], ysend, yrecv, k, at(dy=way))

    def x_piece(a, p, dy):
        k = p * 8 + dy * 2 + a
        return remote(
            arrays[a].at[dy * 2, p], arrays[a].at[dy * 2 + 1, p], xsend, xrecv, k, at(dx=1 if p == 0 else -1)
        )

    def z_weights(m, way):
        rows = (192, 64) if way == 1 else (224, 96)
        return remote(
            W.at[m, pl.ds(rows[0], 32)], W.at[m, pl.ds(rows[1], 32)],
            zsend, zrecv, m * 2 + first(way), at(dz=way),
        )

    def d_own(m):
        return remote(W.at[m, pl.ds(192, 64)], W.at[m, pl.ds(128, 64)], dsend, drecv, m, at(dc=1))

    def d_forward(m):
        return remote(W.at[m, pl.ds(64, 64)], W.at[m, pl.ds(0, 64)], dsend, drecv, 3 + m, at(dc=1))

    both = (1, -1)

    def weights_on(m):
        for way in both:
            z_weights(m, way).wait_recv()
        go(d_forward(m))

    for way in both:
        go(y_piece(0, first(way), way))
    for p in range(2):
        go(x_piece(0, p, 0))
    for way in both:
        go(z_weights(0, way))
    for way in both:
        go(y_piece(0, 1 - first(way), way))
    for p in range(2):
        go(x_piece(1, p, 0))
    for way in both:
        go(y_piece(1, first(way), way))
    for m in (1, 2):
        for way in both:
            go(z_weights(m, way))
    for m in range(3):
        go(d_own(m))
    for way in both:
        y_piece(0, first(way), way).wait_recv()
        go(y_next(0, way))
        go(x_piece(0, first(way), side(way)))
    for way in both:
        go(y_piece(1, 1 - first(way), way))
    for way in both:
        y_piece(0, 1 - first(way), way).wait_recv()
        go(x_piece(0, 1 - first(way), side(way)))
    weights_on(0)
    for way in both:
        y_piece(1, first(way), way).wait_recv()
        go(y_next(1, way))
        go(x_piece(1, first(way), side(way)))
    for way in both:
        y_next(0, way).wait_recv()
        go(x_piece(0, first(way), 2))
    weights_on(1)
    for way in both:
        y_piece(1, 1 - first(way), way).wait_recv()
        go(x_piece(1, 1 - first(way), side(way)))
    for way in both:
        x_piece(1, first(way), side(way)).wait_recv()
        go(y_other(way))
    for m in range(2):
        d_own(m).wait_recv()
        d_forward(m).wait_recv()
    for dy in (0, 3, 1, 2):
        for p in range(2):
            x_piece(0, p, dy).wait_recv()

    def contract(m, a):
        ACC[m] = jnp.zeros((256, 256), F32)

        def step(k, carry):
            cols = pl.ds(pl.multiple_of(k * KC, KC), KC)
            ACC[m] += nt(arrays[a][:, :, :, cols].reshape(256, KC), W[m, :, cols])
            return carry

        lax.fori_loop(0, D // KC, step, 0)

    contract(0, 0)
    contract(1, 0)
    weights_on(2)
    gate, up = ACC[0], ACC[1]
    sig = jax.nn.sigmoid(gate)
    act = gate * sig
    TT[2] = (act * up).T.astype(BF)

    for way in both:
        y_next(1, way).wait_recv()
    for way in both:
        x_piece(1, 1 - first(way), side(way)).wait_recv()
    for p in range(2):
        x_piece(1, p, 0).wait_recv()
    for way in both:
        y_other(way).wait_recv()

    outs = (o_g, o_u, o_d)

    def grad_to_sibling(half, m):
        return remote(SEND.at[half, m], RECV.at[half, m], gsend, grecv, half * 3 + m, at(dc=1))

    def grads(half, m):
        def tile(j, carry):
            cols = pl.ds(pl.multiple_of(j * NC, NC), NC)
            right = arrays[m // 2][:, :, :, cols].reshape(256, NC)
            value = nn(TT[m, pl.ds(half * 128, 128)], right)
            SEND[half, m, :, cols] = value[:64].astype(BF)
            if half:
                outs[m][:, cols] = value[64:]
            else:
                OWNZ[m, :, cols] = value[64:]
            return carry

        lax.fori_loop(0, D // NC, tile, 0)
        go(grad_to_sibling(half, m))

    def grad_over_z(m, way):
        rows = pl.ds(0 if way == -1 else 32, 32)
        return remote(ZSEND.at[m, rows], ZRECV.at[m, rows], zgsend, zgrecv, m * 2 + first(way), at(dz=way))

    def grads_over_z(m):
        grad_to_sibling(0, m).wait_recv()
        ZSEND[m] = (OWNZ[m] + RECV[0, m].astype(F32)).astype(BF)
        for way in both:
            go(grad_over_z(m, way))

    grads(0, 2)

    d_own(2).wait_recv()
    d_forward(2).wait_recv()
    contract(2, 1)
    hidden_grad = ACC[2]
    gate, up = ACC[0], ACC[1]
    sig = jax.nn.sigmoid(gate)
    act = gate * sig
    gate_term = hidden_grad * up * sig * (1.0 + gate * (1.0 - sig))
    up_term = hidden_grad * act
    TERMS[:, :256] = gate_term.astype(BF)
    TERMS[:, 256:] = up_term.astype(BF)
    TT[0] = gate_term.T.astype(BF)
    TT[1] = up_term.T.astype(BF)

    def dx_tile(k, carry):
        cols = pl.ds(pl.multiple_of(k * 256, 256), 256)
        value = nn(TERMS[:, :256], W[0, :, cols]) + nn(TERMS[:, 256:], W[1, :, cols])
        PART[k // 2, k % 2] = value.astype(BF).reshape(4, 2, 32, 256)
        return carry

    def x_hi(dx):
        return ((x + dx) % 4) // 2

    def half_a(h, dy):
        return PART.at[pl.ds(h * 2, 2), :, dy]

    def half_b(h, dx):
        return PART.at[pl.ds(4 + h * 2, 2), x_hi(dx), :, dx % 2]

    def s1_opposite(b, way):
        h = first(way)
        src, where = (half_b(h, 2), at(dx=way)) if b else (half_a(h, 2), at(dy=way))
        return remote(src, (TB if b else TA).at[h], s1send, s1recv, b * 6 + h, where)

    def s1_direct(b, way):
        i, near = first(way), way % 4
        src, where = (half_b(1 - i, near), at(dx=way)) if b else (half_a(1 - i, near), at(dy=way))
        return remote(src, (RB if b else RA).at[i], s1send, s1recv, b * 6 + 2 + i, where)

    def s1_summed(b, way):
        i, near = first(way), way % 4
        src, where = (half_b(i, near), at(dx=way)) if b else (half_a(i, near), at(dy=way))
        return remote(src, (RB if b else RA).at[2 + i], s1send, s1recv, b * 6 + 4 + i, where)

    def s1_sum(b, way):
        h, near = first(way), way % 4
        s1_opposite(b, way).wait_recv()
        mine = half_b(h, near) if b else half_a(h, near)
        mine[...] = (mine[...].astype(F32) + (TB if b else TA)[h].astype(F32)).astype(BF)
        go(s1_summed(b, way))

    def s2a(dx):
        return remote(QA.at[:, x_hi(dx), dx % 2], R2A.at[dx - 1], s2send, s2recv, dx - 1, at(dx=dx))

    def s2b(dy):
        return remote(QB.at[:, dy], R2B.at[dy - 1], s2send, s2recv, 2 + dy, at(dy=dy))

    def s3(dz, dc):
        k = dz * 2 + dc
        return remote(
            F.at[(z + dz) % 8, (c + dc) % 2], R3.at[k], s3send, s3recv, k, at(dz=dz, dc=dc)
        )

    for b in range(2):
        lax.fori_loop(b * 8, b * 8 + 8, dx_tile, 0)
        for way in both:
            go(s1_opposite(b, way))
        for way in both:
            go(s1_direct(b, way))
        if b == 0:
            grads_over_z(2)
    grads(0, 0)
    for way in both:
        s1_sum(0, way)
    grads(0, 1)
    for way in both:
        s1_sum(1, way)
    grads_over_z(0)
    grads_over_z(1)
    for m in (2, 0, 1):
        grads(1, m)

    def s1_total(b):
        for way in both:
            s1_direct(b, way).wait_recv()
        for way in both:
            s1_summed(b, way).wait_recv()
        came = RB if b else RA
        for h in range(2):
            own = half_b(h, 0) if b else half_a(h, 0)
            total = own[...].astype(F32) + came[1 - h].astype(F32) + came[2 + h].astype(F32)
            if b:
                QB[h * 2 : h * 2 + 2] = total.astype(BF)
            else:
                QA[h * 2 : h * 2 + 2] = total.astype(BF)

    s1_total(0)
    for dx in (2, 1, 3):
        go(s2a(dx))
    s1_total(1)
    for dy in (2, 1, 3):
        go(s2b(dy))

    for m in (2, 0, 1):
        grad_to_sibling(1, m).wait_recv()
        outs[m][...] += RECV[1, m].astype(F32)

    for dx in (1, 3, 2):
        s2a(dx).wait_recv()
    total = QA[:, xh, 0].astype(F32)
    for i in range(3):
        total = total + R2A[i].astype(F32)
    F[0:4, 0] = total[:, :, :128].astype(BF)
    F[0:4, 1] = total[:, :, 128:].astype(BF)
    for dy in (1, 3, 2):
        s2b(dy).wait_recv()
    total = QB[:, 0].astype(F32)
    for i in range(3):
        total = total + R2B[i].astype(F32)
    F[4:8, 0] = total[:, :, :128].astype(BF)
    F[4:8, 1] = total[:, :, 128:].astype(BF)
    for dz in (4, 3, 5, 2, 6, 1, 7, 0):
        for dc in range(2):
            if dz or dc:
                go(s3(dz, dc))

    def finish(m):
        for way in both:
            grad_over_z(m, way).wait_recv()
        outs[m][...] = (outs[m][...] + ZRECV[m].astype(F32)) * (1.0 / 32.0)

    finish(2)
    finish(0)
    for dz in range(8):
        for dc in range(2):
            if dz or dc:
                s3(dz, dc).wait_recv()
    for odd in range(2):
        for dc in range(2):
            total = None
            for dz in range(odd, 8, 2):
                if dz == 0 and dc == 0:
                    term = F[z, c].astype(F32)
                else:
                    term = R3[dz * 2 + dc].astype(F32)
                total = term if total is None else total + term
            row = pl.multiple_of(((z + odd) % 2) * 64 + ((c + dc) % 2) * 32, 32)
            o_dx[pl.ds(row, 32), :] = total.astype(BF)
    finish(1)
    for copy in sends:
        copy.wait_send()


def write_out(dx, g, u, d, o_dx, o_g, o_u, o_d, sem):
    copies = [
        pltpu.make_async_copy(src, dst, sem.at[k])
        for k, (src, dst) in enumerate(((g, o_g), (u, o_u), (d, o_d), (dx, o_dx)))
    ]
    for copy in copies:
        copy.start()
    for copy in copies:
        copy.wait()


def body(tokens, cotangent, step_lengths, step_labels, gate_weight, up_weight, down_weight):
    dma = pltpu.SemaphoreType.DMA
    hbm = pl.BlockSpec(memory_space=pltpu.HBM)
    smem = pl.BlockSpec(memory_space=pltpu.SMEM)
    vmem = pl.BlockSpec(memory_space=pltpu.VMEM)
    shapes = [((128, 128), BF)] + [((64, D), F32)] * 3
    held = pl.pallas_call(
        kernel,
        name="ffn_backward",
        out_shape=tuple(pltpu.VMEM(shape, dtype) for shape, dtype in shapes),
        in_specs=[smem, smem] + [hbm] * 5,
        out_specs=[vmem] * 4,
        scratch_shapes=[
            pltpu.VMEM((8, 2, 16, D), BF),
            pltpu.VMEM((8, 2, 16, D), BF),
            pltpu.VMEM((32, D), BF),
            pltpu.VMEM((3, 256, D), BF),
            pltpu.VMEM((3, 256, 256), F32),
            pltpu.VMEM((256, 512), BF),
            pltpu.VMEM((3, 256, 256), BF),
            pltpu.VMEM((2, 3, 64, D), BF),
            pltpu.VMEM((3, 64, D), F32),
            pltpu.VMEM((2, 3, 64, D), BF),
            pltpu.VMEM((3, 64, D), BF),
            pltpu.VMEM((3, 64, D), BF),
            pltpu.VMEM((8, 2, 4, 2, 32, 256), BF),
            pltpu.VMEM((2, 2, 2, 2, 32, 256), BF),
            pltpu.VMEM((2, 2, 4, 32, 256), BF),
            pltpu.VMEM((4, 2, 2, 2, 32, 256), BF),
            pltpu.VMEM((4, 2, 4, 32, 256), BF),
            pltpu.VMEM((4, 2, 2, 32, 256), BF),
            pltpu.VMEM((4, 4, 32, 256), BF),
            pltpu.VMEM((3, 4, 32, 256), BF),
            pltpu.VMEM((3, 4, 32, 256), BF),
            pltpu.VMEM((8, 2, 32, 128), BF),
            pltpu.VMEM((16, 32, 128), BF),
            dma((6,)), dma((16,)), dma((16,)), dma((16,)), dma((16,)),
            dma((6,)), dma((6,)), dma((6,)), dma((6,)),
            dma((6,)), dma((6,)), dma((6,)), dma((6,)),
            dma((12,)), dma((12,)), dma((6,)), dma((6,)), dma((16,)), dma((16,)),
        ],
        compiler_params=pltpu.CompilerParams(
            collective_id=0, has_side_effects=True, vmem_limit_bytes=60 * 2**20 + 2**19
        ),
        cost_estimate=pl.CostEstimate(flops=4_300_000_000, bytes_accessed=8_000_000, transcendentals=65536),
    )(step_lengths, step_labels, tokens, cotangent, gate_weight, up_weight, down_weight)
    return pl.pallas_call(
        write_out,
        name="write_out",
        out_shape=tuple(jax.ShapeDtypeStruct(shape, dtype) for shape, dtype in shapes),
        in_specs=[vmem] * 4,
        out_specs=[hbm] * 4,
        scratch_shapes=[dma((4,))],
    )(*held)


def solution(mesh):
    return jax.shard_map(
        body,
        mesh=mesh,
        in_specs=(
            P("weight", None),
            P("weight", None),
            P("weight", None),
            P("weight", None),
            P(("dp", "weight"), None),
            P(("dp", "weight"), None),
            P(("dp", "weight"), None),
        ),
        out_specs=(
            P("weight", "dp"),
            P(("dp", "weight"), None),
            P(("dp", "weight"), None),
            P(("dp", "weight"), None),
        ),
        check_vma=False,
    )
```

```python
import jax
import jax.numpy as jnp
from jax import lax
from jax.experimental import pallas as pl
from jax.experimental.pallas import tpu as pltpu
from jax.sharding import PartitionSpec as P

MESH = pl.DeviceIdType.MESH
BF = jnp.bfloat16
F32 = jnp.float32
D = 4096
ROWS = 128


def nt(left, right):
    return lax.dot_general(left, right, (((1,), (1,)), ((), ())), preferred_element_type=F32)


def nn(left, right):
    return jnp.dot(left, right, preferred_element_type=F32)


def kernel(
    lens, labs, tok, cot, wg, wu, wd,
    o_dx, o_g, o_u, o_d,
    X, C, CT, W, ACC, TERMS, TT, SEND, OWNZ, RECV, ZSEND, ZRECV,
    PART, TA, TB, RA, RB, QA, QB, R2A, R2B, F, R3,
    in_sem, ysend, yrecv, xsend, xrecv, zsend, zrecv, dsend, drecv,
    gsend, grecv, zgsend, zgrecv, s1send, s1recv, s2send, s2recv, s3send, s3recv,
):
    dp = lax.axis_index("dp")
    wt = lax.axis_index("weight")
    z, xh, c = dp // 4, (dp // 2) % 2, dp % 2
    y, xl = wt // 2, wt % 2
    x = xh * 2 + xl

    def at(dx=0, dy=0, dz=0, dc=0):
        xx = (x + dx) % 4
        yy = (y + dy) % 4
        zz = (z + dz) % 8
        cc = (c + dc) % 2
        return (zz * 4 + (xx // 2) * 2 + cc, yy * 2 + xx % 2)

    def remote(src, dst, ssem, rsem, k, where):
        return pltpu.make_async_remote_copy(
            src_ref=src, dst_ref=dst, send_sem=ssem.at[k], recv_sem=rsem.at[k],
            device_id=where, device_id_type=MESH,
        )

    sends = []

    def go(copy):
        copy.start()
        sends.append(copy)
        return copy

    barrier = pltpu.get_barrier_semaphore()
    partners = [at(dz=dz, dc=dc) for dz in range(8) for dc in range(2) if dz or dc]
    partners += [at(dy=d) for d in (1, 2, 3)] + [at(dx=d) for d in (1, 2, 3)]
    for who in partners:
        pl.semaphore_signal(barrier, inc=1, device_id=who, device_id_type=MESH)

    row0 = pl.multiple_of((z % 2) * 64 + c * 32, 32)
    loads = [pltpu.make_async_copy(cot.at[pl.ds(row0, 32)], CT, in_sem.at[0])]
    for p in range(2):
        loads.append(pltpu.make_async_copy(tok.at[pl.ds(row0 + 16 * p, 16)], X.at[0, p], in_sem.at[1 + p]))
    for m, ref in enumerate((wg, wu, wd)):
        loads.append(pltpu.make_async_copy(ref, W.at[m, pl.ds(192, 64)], in_sem.at[3 + m]))
    for copy in loads:
        copy.start()

    position = lax.broadcasted_iota(jnp.int32, (32, 128), 0) + row0
    segment = jnp.zeros((32, 128), jnp.int32)
    end = lens[0, 0]
    segment = segment + (position >= end).astype(jnp.int32)
    for k in range(1, 4):
        end = end + lens[0, k]
        segment = segment + (position >= end).astype(jnp.int32)
    length = jnp.zeros((32, 128), jnp.int32)
    label = jnp.zeros((32, 128), jnp.int32)
    for k in range(4):
        length = jnp.where(segment == k, lens[0, k], length)
        label = jnp.where(segment == k, labs[0, k], label)
    factor = (1.0 + 2.0 * label.astype(F32)) * lax.rsqrt(length.astype(F32) * 4 / ROWS)
    loads[0].wait()
    for j in range(D // 128):
        cols = slice(j * 128, (j + 1) * 128)
        value = (CT[:, cols].astype(F32) * factor).astype(BF)
        C[0, 0, :, cols] = value[:16]
        C[0, 1, :, cols] = value[16:]
    for copy in loads[1:]:
        copy.wait()
    pl.semaphore_wait(barrier, len(partners))

    arrays = (X, C)

    def first(way):
        return 0 if way == 1 else 1

    def side(way):
        return 3 if way == 1 else 1

    def y_piece(a, p, way):
        k = first(way) * 8 + a * 2 + p
        return remote(arrays[a].at[0, p], arrays[a].at[side(way) * 2, p], ysend, yrecv, k, at(dy=way))

    def y_next(a, way):
        p = first(way)
        k = first(way) * 8 + 4 + a
        return remote(arrays[a].at[side(way) * 2, p], arrays[a].at[4, p], ysend, yrecv, k, at(dy=way))

    def y_other(way):
        p = first(way)
        k = first(way) * 8 + 6
        return remote(C.at[side(way) * 2 + 1, p], C.at[5, p], ysend, yrecv, k, at(dy=way))

    def x_piece(a, p, dy):
        k = p * 8 + dy * 2 + a
        return remote(
            arrays[a].at[dy * 2, p], arrays[a].at[dy * 2 + 1, p], xsend, xrecv, k, at(dx=1 if p == 0 else -1)
        )

    def z_weights(m, way):
        rows = (192, 64) if way == 1 else (224, 96)
        return remote(
            W.at[m, pl.ds(rows[0], 32)], W.at[m, pl.ds(rows[1], 32)],
            zsend, zrecv, m * 2 + first(way), at(dz=way),
        )

    def d_own(m):
        return remote(W.at[m, pl.ds(192, 64)], W.at[m, pl.ds(128, 64)], dsend, drecv, m, at(dc=1))

    def d_forward(m):
        return remote(W.at[m, pl.ds(64, 64)], W.at[m, pl.ds(0, 64)], dsend, drecv, 3 + m, at(dc=1))

    both = (1, -1)

    def weights_on(m):
        for way in both:
            z_weights(m, way).wait_recv()
        go(d_forward(m))

    for way in both:
        go(y_piece(0, first(way), way))
    for p in range(2):
        go(x_piece(0, p, 0))
    for way in both:
        go(z_weights(0, way))
    for way in both:
        go(y_piece(0, 1 - first(way), way))
    for p in range(2):
        go(x_piece(1, p, 0))
    for way in both:
        go(y_piece(1, first(way), way))
    for m in (1, 2):
        for way in both:
            go(z_weights(m, way))
    for m in range(3):
        go(d_own(m))
    for way in both:
        y_piece(0, first(way), way).wait_recv()
        go(y_next(0, way))
        go(x_piece(0, first(way), side(way)))
    for way in both:
        go(y_piece(1, 1 - first(way), way))
    for way in both:
        y_piece(0, 1 - first(way), way).wait_recv()
        go(x_piece(0, 1 - first(way), side(way)))
    weights_on(0)
    for way in both:
        y_piece(1, first(way), way).wait_recv()
        go(y_next(1, way))
        go(x_piece(1, first(way), side(way)))
    for way in both:
        y_next(0, way).wait_recv()
        go(x_piece(0, first(way), 2))
    weights_on(1)
    for way in both:
        y_piece(1, 1 - first(way), way).wait_recv()
        go(x_piece(1, 1 - first(way), side(way)))
    for way in both:
        x_piece(1, first(way), side(way)).wait_recv()
        go(y_other(way))
    weights_on(2)
    for m in range(2):
        d_own(m).wait_recv()
        d_forward(m).wait_recv()
    for dy in (0, 3, 1, 2):
        for p in range(2):
            x_piece(0, p, dy).wait_recv()

    def contract(m, a):
        ACC[m] = nt(arrays[a][...].reshape(256, D), W[m])

    contract(0, 0)
    contract(1, 0)
    gate, up = ACC[0], ACC[1]
    sig = jax.nn.sigmoid(gate)
    act = gate * sig
    TT[2] = (act * up).T.astype(BF)

    for way in both:
        y_next(1, way).wait_recv()
    for way in both:
        x_piece(1, 1 - first(way), side(way)).wait_recv()
    for p in range(2):
        x_piece(1, p, 0).wait_recv()
    for way in both:
        y_other(way).wait_recv()

    outs = (o_g, o_u, o_d)

    def grad_to_sibling(half, m):
        return remote(SEND.at[half, m], RECV.at[half, m], gsend, grecv, half * 3 + m, at(dc=1))

    def grads(half, m):
        value = nn(TT[m, pl.ds(half * 128, 128)], arrays[m // 2][...].reshape(256, D))
        SEND[half, m] = value[:64].astype(BF)
        if half:
            outs[m][...] = value[64:]
        else:
            OWNZ[m] = value[64:]
        go(grad_to_sibling(half, m))

    def grad_over_z(m, way):
        rows = pl.ds(0 if way == -1 else 32, 32)
        return remote(ZSEND.at[m, rows], ZRECV.at[m, rows], zgsend, zgrecv, m * 2 + first(way), at(dz=way))

    def grads_over_z(m):
        grad_to_sibling(0, m).wait_recv()
        ZSEND[m] = (OWNZ[m] + RECV[0, m].astype(F32)).astype(BF)
        for way in both:
            go(grad_over_z(m, way))

    grads(0, 2)

    d_own(2).wait_recv()
    d_forward(2).wait_recv()
    contract(2, 1)
    hidden_grad = ACC[2]
    gate, up = ACC[0], ACC[1]
    sig = jax.nn.sigmoid(gate)
    act = gate * sig
    gate_term = hidden_grad * up * sig * (1.0 + gate * (1.0 - sig))
    up_term = hidden_grad * act
    TERMS[:, :256] = gate_term.astype(BF)
    TERMS[:, 256:] = up_term.astype(BF)
    TT[0] = gate_term.T.astype(BF)
    TT[1] = up_term.T.astype(BF)

    def dx_half(b):
        cols = pl.ds(b * (D // 2), D // 2)
        value = nn(TERMS[...], W[0:2, :, cols].reshape(512, D // 2)).astype(BF)
        for k in range(8):
            PART[b * 4 + k // 2, k % 2] = value[:, k * 256 : (k + 1) * 256].reshape(4, 2, 32, 256)

    def x_hi(dx):
        return ((x + dx) % 4) // 2

    def half_a(h, dy):
        return PART.at[pl.ds(h * 2, 2), :, dy]

    def half_b(h, dx):
        return PART.at[pl.ds(4 + h * 2, 2), x_hi(dx), :, dx % 2]

    def s1_opposite(b, way):
        h = first(way)
        src, where = (half_b(h, 2), at(dx=way)) if b else (half_a(h, 2), at(dy=way))
        return remote(src, (TB if b else TA).at[h], s1send, s1recv, b * 6 + h, where)

    def s1_direct(b, way):
        i, near = first(way), way % 4
        src, where = (half_b(1 - i, near), at(dx=way)) if b else (half_a(1 - i, near), at(dy=way))
        return remote(src, (RB if b else RA).at[i], s1send, s1recv, b * 6 + 2 + i, where)

    def s1_summed(b, way):
        i, near = first(way), way % 4
        src, where = (half_b(i, near), at(dx=way)) if b else (half_a(i, near), at(dy=way))
        return remote(src, (RB if b else RA).at[2 + i], s1send, s1recv, b * 6 + 4 + i, where)

    def s1_sum(b, way):
        h, near = first(way), way % 4
        s1_opposite(b, way).wait_recv()
        mine = half_b(h, near) if b else half_a(h, near)
        mine[...] = (mine[...].astype(F32) + (TB if b else TA)[h].astype(F32)).astype(BF)
        go(s1_summed(b, way))

    def s2a(dx):
        return remote(QA.at[:, x_hi(dx), dx % 2], R2A.at[dx - 1], s2send, s2recv, dx - 1, at(dx=dx))

    def s2b(dy):
        return remote(QB.at[:, dy], R2B.at[dy - 1], s2send, s2recv, 2 + dy, at(dy=dy))

    def s3(dz, dc):
        k = dz * 2 + dc
        return remote(
            F.at[(z + dz) % 8, (c + dc) % 2], R3.at[k], s3send, s3recv, k, at(dz=dz, dc=dc)
        )

    for b in range(2):
        dx_half(b)
        for way in both:
            go(s1_opposite(b, way))
        for way in both:
            go(s1_direct(b, way))
    grads_over_z(2)
    grads(0, 0)
    grads(0, 1)
    for m in (2, 0, 1):
        grads(1, m)
    grads_over_z(0)
    for way in both:
        s1_sum(0, way)
    grads_over_z(1)
    for way in both:
        s1_sum(1, way)

    def s1_total(b):
        for way in both:
            s1_direct(b, way).wait_recv()
        for way in both:
            s1_summed(b, way).wait_recv()
        came = RB if b else RA
        for h in range(2):
            own = half_b(h, 0) if b else half_a(h, 0)
            total = own[...].astype(F32) + came[1 - h].astype(F32) + came[2 + h].astype(F32)
            if b:
                QB[h * 2 : h * 2 + 2] = total.astype(BF)
            else:
                QA[h * 2 : h * 2 + 2] = total.astype(BF)

    s1_total(0)
    for dx in (2, 1, 3):
        go(s2a(dx))
    s1_total(1)
    for dy in (2, 1, 3):
        go(s2b(dy))

    for m in (2, 0, 1):
        grad_to_sibling(1, m).wait_recv()
        outs[m][...] += RECV[1, m].astype(F32)

    for dx in (1, 3, 2):
        s2a(dx).wait_recv()
    total = QA[:, xh, 0].astype(F32)
    for i in range(3):
        total = total + R2A[i].astype(F32)
    F[0:4, 0] = total[:, :, :128].astype(BF)
    F[0:4, 1] = total[:, :, 128:].astype(BF)
    for dy in (1, 3, 2):
        s2b(dy).wait_recv()
    total = QB[:, 0].astype(F32)
    for i in range(3):
        total = total + R2B[i].astype(F32)
    F[4:8, 0] = total[:, :, :128].astype(BF)
    F[4:8, 1] = total[:, :, 128:].astype(BF)
    for dz in (4, 3, 5, 2, 6, 1, 7, 0):
        for dc in range(2):
            if dz or dc:
                go(s3(dz, dc))

    def finish(m):
        for way in both:
            grad_over_z(m, way).wait_recv()
        outs[m][...] = (outs[m][...] + ZRECV[m].astype(F32)) * (1.0 / 32.0)

    finish(2)
    finish(0)
    for dz in range(8):
        for dc in range(2):
            if dz or dc:
                s3(dz, dc).wait_recv()
    for odd in range(2):
        for dc in range(2):
            total = None
            for dz in range(odd, 8, 2):
                if dz == 0 and dc == 0:
                    term = F[z, c].astype(F32)
                else:
                    term = R3[dz * 2 + dc].astype(F32)
                total = term if total is None else total + term
            row = pl.multiple_of(((z + odd) % 2) * 64 + ((c + dc) % 2) * 32, 32)
            o_dx[pl.ds(row, 32), :] = total.astype(BF)
    finish(1)
    for copy in sends:
        copy.wait_send()


def write_out(dx, g, u, d, o_dx, o_g, o_u, o_d, sem):
    copies = [
        pltpu.make_async_copy(src, dst, sem.at[k])
        for k, (src, dst) in enumerate(((g, o_g), (u, o_u), (d, o_d), (dx, o_dx)))
    ]
    for copy in copies:
        copy.start()
    for copy in copies:
        copy.wait()


def body(tokens, cotangent, step_lengths, step_labels, gate_weight, up_weight, down_weight):
    dma = pltpu.SemaphoreType.DMA
    hbm = pl.BlockSpec(memory_space=pltpu.HBM)
    smem = pl.BlockSpec(memory_space=pltpu.SMEM)
    vmem = pl.BlockSpec(memory_space=pltpu.VMEM)
    shapes = [((128, 128), BF)] + [((64, D), F32)] * 3
    held = pl.pallas_call(
        kernel,
        name="ffn_backward",
        out_shape=tuple(pltpu.VMEM(shape, dtype) for shape, dtype in shapes),
        in_specs=[smem, smem] + [hbm] * 5,
        out_specs=[vmem] * 4,
        scratch_shapes=[
            pltpu.VMEM((8, 2, 16, D), BF),
            pltpu.VMEM((8, 2, 16, D), BF),
            pltpu.VMEM((32, D), BF),
            pltpu.VMEM((3, 256, D), BF),
            pltpu.VMEM((3, 256, 256), F32),
            pltpu.VMEM((256, 512), BF),
            pltpu.VMEM((3, 256, 256), BF),
            pltpu.VMEM((2, 3, 64, D), BF),
            pltpu.VMEM((3, 64, D), F32),
            pltpu.VMEM((2, 3, 64, D), BF),
            pltpu.VMEM((3, 64, D), BF),
            pltpu.VMEM((3, 64, D), BF),
            pltpu.VMEM((8, 2, 4, 2, 32, 256), BF),
            pltpu.VMEM((2, 2, 2, 2, 32, 256), BF),
            pltpu.VMEM((2, 2, 4, 32, 256), BF),
            pltpu.VMEM((4, 2, 2, 2, 32, 256), BF),
            pltpu.VMEM((4, 2, 4, 32, 256), BF),
            pltpu.VMEM((4, 2, 2, 32, 256), BF),
            pltpu.VMEM((4, 4, 32, 256), BF),
            pltpu.VMEM((3, 4, 32, 256), BF),
            pltpu.VMEM((3, 4, 32, 256), BF),
            pltpu.VMEM((8, 2, 32, 128), BF),
            pltpu.VMEM((16, 32, 128), BF),
            dma((6,)), dma((16,)), dma((16,)), dma((16,)), dma((16,)),
            dma((6,)), dma((6,)), dma((6,)), dma((6,)),
            dma((6,)), dma((6,)), dma((6,)), dma((6,)),
            dma((12,)), dma((12,)), dma((6,)), dma((6,)), dma((16,)), dma((16,)),
        ],
        compiler_params=pltpu.CompilerParams(
            collective_id=0, has_side_effects=True, vmem_limit_bytes=60 * 2**20 + 2**19
        ),
        cost_estimate=pl.CostEstimate(flops=4_300_000_000, bytes_accessed=8_000_000, transcendentals=65536),
    )(step_lengths, step_labels, tokens, cotangent, gate_weight, up_weight, down_weight)
    return pl.pallas_call(
        write_out,
        name="write_out",
        out_shape=tuple(jax.ShapeDtypeStruct(shape, dtype) for shape, dtype in shapes),
        in_specs=[vmem] * 4,
        out_specs=[hbm] * 4,
        scratch_shapes=[dma((4,))],
        compiler_params=pltpu.CompilerParams(vmem_limit_bytes=2**20),
    )(*held)


def solution(mesh):
    return jax.shard_map(
        body,
        mesh=mesh,
        in_specs=(
            P("weight", None),
            P("weight", None),
            P("weight", None),
            P("weight", None),
            P(("dp", "weight"), None),
            P(("dp", "weight"), None),
            P(("dp", "weight"), None),
        ),
        out_specs=(
            P("weight", "dp"),
            P(("dp", "weight"), None),
            P(("dp", "weight"), None),
            P(("dp", "weight"), None),
        ),
        check_vma=False,
    )
```

```python
import jax
import jax.numpy as jnp
from jax import lax
from jax.experimental import pallas as pl
from jax.experimental.pallas import tpu as pltpu
from jax.sharding import PartitionSpec as P

MESH = pl.DeviceIdType.MESH
BF = jnp.bfloat16
F32 = jnp.float32
D = 4096
HALF = D // 2
ROWS = 128


def nt(left, right):
    return lax.dot_general(left, right, (((1,), (1,)), ((), ())), preferred_element_type=F32)


def nn(left, right):
    return jnp.dot(left, right, preferred_element_type=F32)


def kernel(
    lens, labs, tok, cot, wg, wu, wd,
    o_dx, o_g, o_u, o_d,
    X, C, CT, W, ACC, TERMS, TT, SEND, OWNZ, RECV, ZSEND, ZRECV,
    PART, TA, TB, RA, RB, QA, QB, R2A, R2B, F, R3,
    in_sem, ysend, yrecv, xsend, xrecv, zsend, zrecv, dsend, drecv,
    gsend, grecv, zgsend, zgrecv, s1send, s1recv, s2send, s2recv, s3send, s3recv, there,
):
    dp = lax.axis_index("dp")
    wt = lax.axis_index("weight")
    z, xh, c = dp // 4, (dp // 2) % 2, dp % 2
    y, xl = wt // 2, wt % 2
    x = xh * 2 + xl

    def at(dx=0, dy=0, dz=0, dc=0):
        xx = (x + dx) % 4
        yy = (y + dy) % 4
        zz = (z + dz) % 8
        cc = (c + dc) % 2
        return (zz * 4 + (xx // 2) * 2 + cc, yy * 2 + xx % 2)

    def remote(src, dst, ssem, rsem, k, where):
        return pltpu.make_async_remote_copy(
            src_ref=src, dst_ref=dst, send_sem=ssem.at[k], recv_sem=rsem.at[k],
            device_id=where, device_id_type=MESH,
        )

    sends = []

    def go(copy):
        copy.start()
        sends.append(copy)
        return copy

    barrier = pltpu.get_barrier_semaphore()
    column = [at(dc=1), at(dz=1), at(dz=-1)]
    partners = column + [at(dy=1), at(dy=-1), at(dx=1), at(dx=-1)]
    for who in partners:
        pl.semaphore_signal(barrier, inc=1, device_id=who, device_id_type=MESH)

    def tell(r):
        for who in column:
            pl.semaphore_signal(there.at[r], inc=1, device_id=who, device_id_type=MESH)

    def told(r):
        pl.semaphore_wait(there.at[r], len(column))

    row0 = pl.multiple_of((z % 2) * 64 + c * 32, 32)
    loads = [pltpu.make_async_copy(cot.at[pl.ds(row0, 32)], CT, in_sem.at[0])]
    for p in range(2):
        loads.append(pltpu.make_async_copy(tok.at[pl.ds(row0 + 16 * p, 16)], X.at[0, p], in_sem.at[1 + p]))
    for m, ref in enumerate((wg, wu, wd)):
        loads.append(pltpu.make_async_copy(ref, W.at[m, pl.ds(192, 64)], in_sem.at[3 + m]))
    for copy in loads:
        copy.start()

    for copy in loads[1:]:
        copy.wait()
    pl.semaphore_wait(barrier, len(partners))

    def first(way):
        return 0 if way == 1 else 1

    def side(way):
        return 3 if way == 1 else 1

    def part(a, slot, p):
        return C.at[slot, p, :, pl.ds((a - 1) * HALF, HALF)] if a else X.at[slot, p]

    def y_piece(a, p, way):
        k = first(way) * 11 + a * 2 + p
        return remote(part(a, 0, p), part(a, side(way) * 2, p), ysend, yrecv, k, at(dy=way))

    def y_next(a, way):
        p = first(way)
        k = first(way) * 11 + 6 + a
        return remote(part(a, side(way) * 2, p), part(a, 4, p), ysend, yrecv, k, at(dy=way))

    def y_other(a, way):
        p = first(way)
        k = first(way) * 11 + 8 + a
        return remote(part(a, side(way) * 2 + 1, p), part(a, 5, p), ysend, yrecv, k, at(dy=way))

    def x_piece(a, p, dy):
        k = p * 12 + dy * 3 + a
        return remote(
            part(a, dy * 2, p), part(a, dy * 2 + 1, p), xsend, xrecv, k, at(dx=1 if p == 0 else -1)
        )

    def z_weights(m, way):
        rows = (192, 64) if way == 1 else (224, 96)
        return remote(
            W.at[m, pl.ds(rows[0], 32)], W.at[m, pl.ds(rows[1], 32)],
            zsend, zrecv, m * 2 + first(way), at(dz=way),
        )

    def d_own(m):
        return remote(W.at[m, pl.ds(192, 64)], W.at[m, pl.ds(128, 64)], dsend, drecv, m, at(dc=1))

    def d_forward(m):
        return remote(W.at[m, pl.ds(64, 64)], W.at[m, pl.ds(0, 64)], dsend, drecv, 3 + m, at(dc=1))

    both = (1, -1)

    def weights_on(m):
        for way in both:
            z_weights(m, way).wait_recv()
        go(d_forward(m))

    for way in both:
        go(y_piece(0, first(way), way))
    for p in range(2):
        go(x_piece(0, p, 0))
    for m in range(3):
        for way in both:
            go(z_weights(m, way))
        if m == 0:
            for way in both:
                go(y_piece(0, 1 - first(way), way))
    for m in range(3):
        go(d_own(m))
    tell(0)

    position = lax.broadcasted_iota(jnp.int32, (32, 128), 0) + row0
    segment = jnp.zeros((32, 128), jnp.int32)
    end = lens[0, 0]
    segment = segment + (position >= end).astype(jnp.int32)
    for k in range(1, 4):
        end = end + lens[0, k]
        segment = segment + (position >= end).astype(jnp.int32)
    length = jnp.zeros((32, 128), jnp.int32)
    label = jnp.zeros((32, 128), jnp.int32)
    for k in range(4):
        length = jnp.where(segment == k, lens[0, k], length)
        label = jnp.where(segment == k, labs[0, k], label)
    factor = (1.0 + 2.0 * label.astype(F32)) * lax.rsqrt(length.astype(F32) * 4 / ROWS)
    loads[0].wait()
    for j in range(D // 128):
        cols = slice(j * 128, (j + 1) * 128)
        value = (CT[:, cols].astype(F32) * factor).astype(BF)
        C[0, 0, :, cols] = value[:16]
        C[0, 1, :, cols] = value[16:]
    for a in (1, 2):
        for p in range(2):
            go(x_piece(a, p, 0))
        for way in both:
            go(y_piece(a, first(way), way))
    for way in both:
        y_piece(0, first(way), way).wait_recv()
        go(y_next(0, way))
        go(x_piece(0, first(way), side(way)))
    for a in (1, 2):
        for way in both:
            go(y_piece(a, 1 - first(way), way))
    for way in both:
        y_piece(0, 1 - first(way), way).wait_recv()
        go(x_piece(0, 1 - first(way), side(way)))
    weights_on(0)
    told(0)
    tell(1)
    for a in (1, 2):
        for way in both:
            y_piece(a, first(way), way).wait_recv()
            go(x_piece(a, first(way), side(way)))
            go(y_next(a, way))
    for way in both:
        y_next(0, way).wait_recv()
        go(x_piece(0, first(way), 2))
    weights_on(1)
    told(1)
    tell(2)
    for a in (1, 2):
        for way in both:
            y_piece(a, 1 - first(way), way).wait_recv()
            go(x_piece(a, 1 - first(way), side(way)))
        for way in both:
            x_piece(a, first(way), side(way)).wait_recv()
            go(y_other(a, way))
    weights_on(2)
    told(2)
    tell(3)

    def contract(m, ref):
        ACC[m] = nt(ref[...].reshape(256, D), W[m])

    for m in range(2):
        d_own(m).wait_recv()
        d_forward(m).wait_recv()
    for dy in (0, 3, 1, 2):
        for p in range(2):
            x_piece(0, p, dy).wait_recv()
    contract(0, X)
    contract(1, X)
    gate, up = ACC[0], ACC[1]
    sig = jax.nn.sigmoid(gate)
    act = gate * sig
    TT[2] = (act * up).T.astype(BF)

    def weighted_here(a):
        for way in both:
            y_next(a, way).wait_recv()
        for way in both:
            x_piece(a, 1 - first(way), side(way)).wait_recv()
        for p in range(2):
            x_piece(a, p, 0).wait_recv()
        for way in both:
            y_other(a, way).wait_recv()

    outs = (o_g, o_u, o_d)

    def block_of(ref, h):
        return ref if h is None else ref.at[:, pl.ds(h * HALF, HALF)]

    def grad_to_sibling(half, m, h=None):
        k = half * 3 + m if h != 1 else 6
        return remote(
            block_of(SEND.at[half, m], h), block_of(RECV.at[half, m], h), gsend, grecv, k, at(dc=1)
        )

    def grads(half, m, h=None):
        if m == 2:
            right = C[...] if h is None else C[:, :, :, h * HALF : (h + 1) * HALF]
        else:
            right = X[...]
        value = nn(TT[m, pl.ds(half * 128, 128)], right.reshape(256, right.shape[-1]))
        block_of(SEND.at[half, m], h)[...] = value[:64].astype(BF)
        block_of(outs[m] if half else OWNZ.at[m], h)[...] = value[64:]
        go(grad_to_sibling(half, m, h))

    def grad_over_z(m, way, h=None):
        rows = pl.ds(0 if way == -1 else 32, 32)
        k = (m if h != 1 else 3) * 2 + first(way)
        return remote(
            block_of(ZSEND.at[m, rows], h), block_of(ZRECV.at[m, rows], h), zgsend, zgrecv, k, at(dz=way)
        )

    def grads_over_z(m, h=None):
        grad_to_sibling(0, m, h).wait_recv()
        mine, came = block_of(OWNZ.at[m], h), block_of(RECV.at[0, m], h)
        block_of(ZSEND.at[m], h)[...] = (mine[...] + came[...].astype(F32)).astype(BF)
        for way in both:
            go(grad_over_z(m, way, h))

    weighted_here(1)
    grads(0, 2, 0)
    weighted_here(2)
    d_own(2).wait_recv()
    d_forward(2).wait_recv()
    contract(2, C)
    grads(0, 2, 1)
    grads_over_z(2, 0)
    hidden_grad = ACC[2]
    gate, up = ACC[0], ACC[1]
    sig = jax.nn.sigmoid(gate)
    act = gate * sig
    gate_term = hidden_grad * up * sig * (1.0 + gate * (1.0 - sig))
    up_term = hidden_grad * act
    TERMS[:, :256] = gate_term.astype(BF)
    TERMS[:, 256:] = up_term.astype(BF)
    TT[0] = gate_term.T.astype(BF)
    TT[1] = up_term.T.astype(BF)

    def dx_half(b):
        cols = pl.ds(b * (D // 2), D // 2)
        value = nn(TERMS[...], W[0:2, :, cols].reshape(512, D // 2)).astype(BF)
        for k in range(8):
            PART[b * 4 + k // 2, k % 2] = value[:, k * 256 : (k + 1) * 256].reshape(4, 2, 32, 256)

    def x_hi(dx):
        return ((x + dx) % 4) // 2

    def jz(j):
        return (z + j) % 2

    def chunk(b, h, to, j):
        if b:
            return PART.at[4 + h * 2 + jz(j), x_hi(to), :, to % 2]
        return PART.at[h * 2 + jz(j), :, to]

    def along(b, way):
        return at(dx=way) if b else at(dy=way)

    def s1_opposite(b, way, j):
        h = first(way)
        return remote(chunk(b, h, 2, j), (TB if b else TA).at[j, h], s1send, s1recv, b * 12 + j * 6 + h, along(b, way))

    def s1_direct(b, way, j):
        i = first(way)
        return remote(
            chunk(b, 1 - i, way % 4, j), (RB if b else RA).at[j, i],
            s1send, s1recv, b * 12 + j * 6 + 2 + i, along(b, way),
        )

    def s1_summed(b, way, j):
        i = first(way)
        return remote(
            chunk(b, i, way % 4, j), (RB if b else RA).at[j, 2 + i],
            s1send, s1recv, b * 12 + j * 6 + 4 + i, along(b, way),
        )

    def s1_sum(b, j):
        for way in both:
            h = first(way)
            s1_opposite(b, way, j).wait_recv()
            mine = chunk(b, h, way % 4, j)
            mine[...] = (mine[...].astype(F32) + (TB if b else TA)[j, h].astype(F32)).astype(BF)
            go(s1_summed(b, way, j))
        if j == 0:
            for way in both:
                go(s1_direct(b, way, 1))

    def s1_total(b, j):
        for way in both:
            s1_direct(b, way, j).wait_recv()
        for way in both:
            s1_summed(b, way, j).wait_recv()
        came = RB if b else RA
        for h in range(2):
            total = chunk(b, h, 0, j)[...].astype(F32) + came[j, 1 - h].astype(F32) + came[j, 2 + h].astype(F32)
            (QB if b else QA)[j, h] = total.astype(BF)
        for d in (2, 1, 3):
            go(s2(b, d, j))

    def s2(b, d, j):
        if b:
            src, dst, where = QB.at[j, :, d], R2B.at[d - 1, j], at(dy=d)
        else:
            src, dst, where = QA.at[j, :, x_hi(d), d % 2], R2A.at[d - 1, j], at(dx=d)
        return remote(src, dst, s2send, s2recv, b * 6 + j * 3 + d - 1, where)

    def s2_total(b, j):
        for d in (1, 3, 2):
            s2(b, d, j).wait_recv()
        if b:
            total, came = QB[j, :, 0].astype(F32), R2B
        else:
            total, came = QA[j, :, xh, 0].astype(F32), R2A
        for i in range(3):
            total = total + came[i, j].astype(F32)
        for h in range(2):
            for k in range(2):
                F[b * 4 + h * 2 + jz(j), k] = total[h, :, k * 128 : (k + 1) * 128].astype(BF)

    def s3(dz, dc):
        k = dz * 2 + dc
        return remote(
            F.at[(z + dz) % 8, (c + dc) % 2], R3.at[k], s3send, s3recv, k, at(dz=dz, dc=dc)
        )

    for b in range(2):
        dx_half(b)
        for j in range(2):
            for way in both:
                go(s1_opposite(b, way, j))
        for way in both:
            go(s1_direct(b, way, 0))
    grads_over_z(2, 1)
    grads(0, 0)
    grads(0, 1)
    grads(1, 2)
    s1_sum(0, 0)
    s1_sum(1, 0)
    grads_over_z(0)
    grads(1, 0)
    s1_sum(0, 1)
    s1_sum(1, 1)
    grads_over_z(1)
    grads(1, 1)
    for j in range(2):
        for b in range(2):
            s1_total(b, j)

    for m in (2, 0, 1):
        grad_to_sibling(1, m).wait_recv()
        outs[m][...] += RECV[1, m].astype(F32)

    told(3)
    before = len(sends)
    for j in range(2):
        for b in range(2):
            s2_total(b, j)
        for dz in (4, 3, 5, 2, 6, 1, 7, 0):
            for dc in range(2):
                if dz % 2 == j and (dz or dc):
                    go(s3(dz, dc))
    for copy in sends[:before]:
        copy.wait_send()

    def finish(m):
        for way in both:
            for h in (0, 1) if m == 2 else (None,):
                grad_over_z(m, way, h).wait_recv()
        outs[m][...] = (outs[m][...] + ZRECV[m].astype(F32)) * (1.0 / 32.0)

    finish(2)
    finish(0)
    finish(1)
    for dz in range(8):
        for dc in range(2):
            if dz or dc:
                s3(dz, dc).wait_recv()
    for odd in range(2):
        for dc in range(2):
            total = None
            for dz in range(odd, 8, 2):
                if dz == 0 and dc == 0:
                    term = F[z, c].astype(F32)
                else:
                    term = R3[dz * 2 + dc].astype(F32)
                total = term if total is None else total + term
            row = pl.multiple_of(((z + odd) % 2) * 64 + ((c + dc) % 2) * 32, 32)
            o_dx[pl.ds(row, 32), :] = total.astype(BF)
    for copy in sends[before:]:
        copy.wait_send()


def write_out(dx, g, u, d, o_dx, o_g, o_u, o_d, sem):
    copies = [
        pltpu.make_async_copy(src, dst, sem.at[k])
        for k, (src, dst) in enumerate(((g, o_g), (u, o_u), (d, o_d), (dx, o_dx)))
    ]
    for copy in copies:
        copy.start()
    for copy in copies:
        copy.wait()


def body(tokens, cotangent, step_lengths, step_labels, gate_weight, up_weight, down_weight):
    dma = pltpu.SemaphoreType.DMA
    hbm = pl.BlockSpec(memory_space=pltpu.HBM)
    smem = pl.BlockSpec(memory_space=pltpu.SMEM)
    vmem = pl.BlockSpec(memory_space=pltpu.VMEM)
    shapes = [((128, 128), BF)] + [((64, D), F32)] * 3
    held = pl.pallas_call(
        kernel,
        name="ffn_backward",
        out_shape=tuple(pltpu.VMEM(shape, dtype) for shape, dtype in shapes),
        in_specs=[smem, smem] + [hbm] * 5,
        out_specs=[vmem] * 4,
        scratch_shapes=[
            pltpu.VMEM((8, 2, 16, D), BF),
            pltpu.VMEM((8, 2, 16, D), BF),
            pltpu.VMEM((32, D), BF),
            pltpu.VMEM((3, 256, D), BF),
            pltpu.VMEM((3, 256, 256), F32),
            pltpu.VMEM((256, 512), BF),
            pltpu.VMEM((3, 256, 256), BF),
            pltpu.VMEM((2, 3, 64, D), BF),
            pltpu.VMEM((3, 64, D), F32),
            pltpu.VMEM((2, 3, 64, D), BF),
            pltpu.VMEM((3, 64, D), BF),
            pltpu.VMEM((3, 64, D), BF),
            pltpu.VMEM((8, 2, 4, 2, 32, 256), BF),
            pltpu.VMEM((2, 2, 2, 2, 32, 256), BF),
            pltpu.VMEM((2, 2, 4, 32, 256), BF),
            pltpu.VMEM((2, 4, 2, 2, 32, 256), BF),
            pltpu.VMEM((2, 4, 4, 32, 256), BF),
            pltpu.VMEM((2, 2, 2, 2, 32, 256), BF),
            pltpu.VMEM((2, 2, 4, 32, 256), BF),
            pltpu.VMEM((3, 2, 2, 32, 256), BF),
            pltpu.VMEM((3, 2, 2, 32, 256), BF),
            pltpu.VMEM((8, 2, 32, 128), BF),
            pltpu.VMEM((16, 32, 128), BF),
            dma((6,)), dma((22,)), dma((22,)), dma((24,)), dma((24,)),
            dma((6,)), dma((6,)), dma((6,)), dma((6,)),
            dma((7,)), dma((7,)), dma((8,)), dma((8,)),
            dma((24,)), dma((24,)), dma((12,)), dma((12,)), dma((16,)), dma((16,)),
            pltpu.SemaphoreType.REGULAR((4,)),
        ],
        compiler_params=pltpu.CompilerParams(
            collective_id=0, has_side_effects=True, vmem_limit_bytes=60 * 2**20 + 2**19
        ),
        cost_estimate=pl.CostEstimate(flops=4_300_000_000, bytes_accessed=8_000_000, transcendentals=65536),
    )(step_lengths, step_labels, tokens, cotangent, gate_weight, up_weight, down_weight)
    return pl.pallas_call(
        write_out,
        name="write_out",
        out_shape=tuple(jax.ShapeDtypeStruct(shape, dtype) for shape, dtype in shapes),
        in_specs=[vmem] * 4,
        out_specs=[hbm] * 4,
        scratch_shapes=[dma((4,))],
        compiler_params=pltpu.CompilerParams(vmem_limit_bytes=2**20),
    )(*held)


def solution(mesh):
    return jax.shard_map(
        body,
        mesh=mesh,
        in_specs=(
            P("weight", None),
            P("weight", None),
            P("weight", None),
            P("weight", None),
            P(("dp", "weight"), None),
            P(("dp", "weight"), None),
            P(("dp", "weight"), None),
        ),
        out_specs=(
            P("weight", "dp"),
            P(("dp", "weight"), None),
            P(("dp", "weight"), None),
            P(("dp", "weight"), None),
        ),
        check_vma=False,
    )
```

```python
import jax
import jax.numpy as jnp
from jax import lax
from jax.experimental import pallas as pl
from jax.experimental.pallas import tpu as pltpu
from jax.sharding import PartitionSpec as P

MESH = pl.DeviceIdType.MESH
BF = jnp.bfloat16
F32 = jnp.float32
D = 4096
HALF = D // 2
EARLY = 1024
ROWS = 128


def nt(left, right):
    return lax.dot_general(left, right, (((1,), (1,)), ((), ())), preferred_element_type=F32)


def nn(left, right):
    return jnp.dot(left, right, preferred_element_type=F32)


def kernel(
    lens, labs, tok, cot, wg, wu, wd,
    o_dx, o_g, o_u, o_d,
    X, C, CT, W, ACC, TERMS, TT, SEND, OWNZ, RECV, ZSEND, ZRECV, EARLYS, EARLYR,
    PART, TA, TB, RA, RB, QA, QB, R2A, R2B, F, R3,
    in_sem, ysend, yrecv, xsend, xrecv, zsend, zrecv, dsend, drecv,
    gsend, grecv, zgsend, zgrecv, s1send, s1recv, s2send, s2recv, s3send, s3recv, esend, erecv, there,
):
    dp = lax.axis_index("dp")
    wt = lax.axis_index("weight")
    z, xh, c = dp // 4, (dp // 2) % 2, dp % 2
    y, xl = wt // 2, wt % 2
    x = xh * 2 + xl

    def at(dx=0, dy=0, dz=0, dc=0):
        xx = (x + dx) % 4
        yy = (y + dy) % 4
        zz = (z + dz) % 8
        cc = (c + dc) % 2
        return (zz * 4 + (xx // 2) * 2 + cc, yy * 2 + xx % 2)

    def remote(src, dst, ssem, rsem, k, where):
        return pltpu.make_async_remote_copy(
            src_ref=src, dst_ref=dst, send_sem=ssem.at[k], recv_sem=rsem.at[k],
            device_id=where, device_id_type=MESH,
        )

    sends = []

    def go(copy):
        copy.start()
        sends.append(copy)
        return copy

    barrier = pltpu.get_barrier_semaphore()
    column = [at(dc=1), at(dz=1), at(dz=-1)]
    partners = column + [at(dy=1), at(dy=-1), at(dx=1), at(dx=-1)]
    for who in partners:
        pl.semaphore_signal(barrier, inc=1, device_id=who, device_id_type=MESH)

    def tell(r):
        for who in column:
            pl.semaphore_signal(there.at[r], inc=1, device_id=who, device_id_type=MESH)

    def told(r):
        pl.semaphore_wait(there.at[r], len(column))

    row0 = pl.multiple_of((z % 2) * 64 + c * 32, 32)
    loads = [pltpu.make_async_copy(cot.at[pl.ds(row0, 32)], CT, in_sem.at[0])]
    for p in range(2):
        loads.append(pltpu.make_async_copy(tok.at[pl.ds(row0 + 16 * p, 16)], X.at[0, p], in_sem.at[1 + p]))
    for m, ref in enumerate((wg, wu, wd)):
        loads.append(pltpu.make_async_copy(ref, W.at[m, pl.ds(192, 64)], in_sem.at[3 + m]))
    for copy in loads:
        copy.start()

    for copy in loads[1:]:
        copy.wait()
    pl.semaphore_wait(barrier, len(partners))

    def first(way):
        return 0 if way == 1 else 1

    def side(way):
        return 3 if way == 1 else 1

    def part(a, slot, p):
        return C.at[slot, p, :, pl.ds((a - 1) * HALF, HALF)] if a else X.at[slot, p]

    def y_piece(a, p, way):
        k = first(way) * 11 + a * 2 + p
        return remote(part(a, 0, p), part(a, side(way) * 2, p), ysend, yrecv, k, at(dy=way))

    def y_next(a, way):
        p = first(way)
        k = first(way) * 11 + 6 + a
        return remote(part(a, side(way) * 2, p), part(a, 4, p), ysend, yrecv, k, at(dy=way))

    def y_other(a, way):
        p = first(way)
        k = first(way) * 11 + 8 + a
        return remote(part(a, side(way) * 2 + 1, p), part(a, 5, p), ysend, yrecv, k, at(dy=way))

    def x_piece(a, p, dy):
        k = p * 12 + dy * 3 + a
        return remote(
            part(a, dy * 2, p), part(a, dy * 2 + 1, p), xsend, xrecv, k, at(dx=1 if p == 0 else -1)
        )

    def z_weights(m, way):
        rows = (192, 64) if way == 1 else (224, 96)
        return remote(
            W.at[m, pl.ds(rows[0], 32)], W.at[m, pl.ds(rows[1], 32)],
            zsend, zrecv, m * 2 + first(way), at(dz=way),
        )

    def d_own(m):
        return remote(W.at[m, pl.ds(192, 64)], W.at[m, pl.ds(128, 64)], dsend, drecv, m, at(dc=1))

    def d_forward(m):
        return remote(W.at[m, pl.ds(64, 64)], W.at[m, pl.ds(0, 64)], dsend, drecv, 3 + m, at(dc=1))

    both = (1, -1)

    def weights_on(m):
        for way in both:
            z_weights(m, way).wait_recv()
        go(d_forward(m))

    for way in both:
        go(y_piece(0, first(way), way))
    for p in range(2):
        go(x_piece(0, p, 0))
    for m in range(3):
        for way in both:
            go(z_weights(m, way))
        if m == 0:
            for way in both:
                go(y_piece(0, 1 - first(way), way))
    for m in range(3):
        go(d_own(m))
    tell(0)

    position = lax.broadcasted_iota(jnp.int32, (32, 128), 0) + row0
    segment = jnp.zeros((32, 128), jnp.int32)
    end = lens[0, 0]
    segment = segment + (position >= end).astype(jnp.int32)
    for k in range(1, 4):
        end = end + lens[0, k]
        segment = segment + (position >= end).astype(jnp.int32)
    length = jnp.zeros((32, 128), jnp.int32)
    label = jnp.zeros((32, 128), jnp.int32)
    for k in range(4):
        length = jnp.where(segment == k, lens[0, k], length)
        label = jnp.where(segment == k, labs[0, k], label)
    factor = (1.0 + 2.0 * label.astype(F32)) * lax.rsqrt(length.astype(F32) * 4 / ROWS)
    loads[0].wait()
    for j in range(D // 128):
        cols = slice(j * 128, (j + 1) * 128)
        value = (CT[:, cols].astype(F32) * factor).astype(BF)
        C[0, 0, :, cols] = value[:16]
        C[0, 1, :, cols] = value[16:]
    for a in (1, 2):
        for p in range(2):
            go(x_piece(a, p, 0))
        for way in both:
            go(y_piece(a, first(way), way))
    for way in both:
        y_piece(0, first(way), way).wait_recv()
        go(y_next(0, way))
        go(x_piece(0, first(way), side(way)))
    for a in (1, 2):
        for way in both:
            go(y_piece(a, 1 - first(way), way))
    for way in both:
        y_piece(0, 1 - first(way), way).wait_recv()
        go(x_piece(0, 1 - first(way), side(way)))
    weights_on(0)
    told(0)
    tell(1)
    for a in (1, 2):
        for way in both:
            y_piece(a, first(way), way).wait_recv()
            go(x_piece(a, first(way), side(way)))
            go(y_next(a, way))
    for way in both:
        y_next(0, way).wait_recv()
        go(x_piece(0, first(way), 2))
    weights_on(1)
    told(1)
    tell(2)
    for a in (1, 2):
        for way in both:
            y_piece(a, 1 - first(way), way).wait_recv()
            go(x_piece(a, 1 - first(way), side(way)))
        for way in both:
            x_piece(a, first(way), side(way)).wait_recv()
            go(y_other(a, way))
    weights_on(2)
    told(2)
    tell(3)

    def contract(m, ref):
        ACC[m] = nt(ref[...].reshape(256, D), W[m])

    for m in range(2):
        d_own(m).wait_recv()
        d_forward(m).wait_recv()
    for dy in (0, 3, 1, 2):
        for p in range(2):
            x_piece(0, p, dy).wait_recv()
    contract(0, X)
    contract(1, X)
    gate, up = ACC[0], ACC[1]
    sig = jax.nn.sigmoid(gate)
    act = gate * sig
    TT[2] = (act * up).T.astype(BF)

    def weighted_here(a):
        for way in both:
            y_next(a, way).wait_recv()
        for way in both:
            x_piece(a, 1 - first(way), side(way)).wait_recv()
        for p in range(2):
            x_piece(a, p, 0).wait_recv()
        for way in both:
            y_other(a, way).wait_recv()

    outs = (o_g, o_u, o_d)

    def block_of(ref, h):
        if h is None:
            return ref
        return ref.at[:, EARLY:HALF] if h == 0 else ref.at[:, HALF:]

    def grad_to_sibling(half, m, h=None):
        k = half * 3 + m if h != 1 else 6
        return remote(
            block_of(SEND.at[half, m], h), block_of(RECV.at[half, m], h), gsend, grecv, k, at(dc=1)
        )

    def early_over_z(way, other):
        row = 0 if way == -1 else 32
        return remote(
            EARLYS.at[pl.ds((64 if other == 0 else 0) + row, 32)], EARLYR.at[other, pl.ds(row, 32)],
            esend, erecv, first(way) * 2 + other, at(dz=way, dc=other),
        )

    def grads(half, m, h=None):
        if m == 2:
            right = C[...] if h is None else C[:, :, :, h * HALF : (h + 1) * HALF]
        else:
            right = X[...]
        value = nn(TT[m, pl.ds(half * 128, 128)], right.reshape(256, right.shape[-1]))
        if h == 0:
            EARLYS[...] = value[:, :EARLY].astype(BF)
            for way in both:
                for other in (1, 0):
                    go(early_over_z(way, other))
            value = value[:, EARLY:]
        block_of(SEND.at[half, m], h)[...] = value[:64].astype(BF)
        block_of(outs[m] if half else OWNZ.at[m], h)[...] = value[64:]
        go(grad_to_sibling(half, m, h))

    def grad_over_z(m, way, h=None):
        rows = pl.ds(0 if way == -1 else 32, 32)
        k = (m if h != 1 else 3) * 2 + first(way)
        return remote(
            block_of(ZSEND.at[m, rows], h), block_of(ZRECV.at[m, rows], h), zgsend, zgrecv, k, at(dz=way)
        )

    def grads_over_z(m, h=None):
        grad_to_sibling(0, m, h).wait_recv()
        mine, came = block_of(OWNZ.at[m], h), block_of(RECV.at[0, m], h)
        block_of(ZSEND.at[m], h)[...] = (mine[...] + came[...].astype(F32)).astype(BF)
        for way in both:
            go(grad_over_z(m, way, h))

    weighted_here(1)
    grads(0, 2, 0)
    weighted_here(2)
    d_own(2).wait_recv()
    d_forward(2).wait_recv()
    contract(2, C)
    grads(0, 2, 1)
    grads_over_z(2, 0)
    hidden_grad = ACC[2]
    gate, up = ACC[0], ACC[1]
    sig = jax.nn.sigmoid(gate)
    act = gate * sig
    gate_term = hidden_grad * up * sig * (1.0 + gate * (1.0 - sig))
    up_term = hidden_grad * act
    TERMS[:, :256] = gate_term.astype(BF)
    TERMS[:, 256:] = up_term.astype(BF)

    def dx_part(b, j):
        for h in range(2):
            place = b * 4 + h * 2 + jz(j)
            cols = pl.ds(pl.multiple_of(place * 512, 512), 512)
            value = nn(TERMS[...], W[0:2, :, cols].reshape(512, 512)).astype(BF)
            for k in range(2):
                PART[place, k] = value[:, k * 256 : (k + 1) * 256].reshape(4, 2, 32, 256)

    def x_hi(dx):
        return ((x + dx) % 4) // 2

    def jz(j):
        return (z + j) % 2

    def chunk(b, h, to, j):
        if b:
            return PART.at[4 + h * 2 + jz(j), x_hi(to), :, to % 2]
        return PART.at[h * 2 + jz(j), :, to]

    def along(b, way):
        return at(dx=way) if b else at(dy=way)

    def s1_opposite(b, way, j):
        h = first(way)
        return remote(chunk(b, h, 2, j), (TB if b else TA).at[j, h], s1send, s1recv, b * 12 + j * 6 + h, along(b, way))

    def s1_direct(b, way, j):
        i = first(way)
        return remote(
            chunk(b, 1 - i, way % 4, j), (RB if b else RA).at[j, i],
            s1send, s1recv, b * 12 + j * 6 + 2 + i, along(b, way),
        )

    def s1_summed(b, way, j):
        i = first(way)
        return remote(
            chunk(b, i, way % 4, j), (RB if b else RA).at[j, 2 + i],
            s1send, s1recv, b * 12 + j * 6 + 4 + i, along(b, way),
        )

    def s1_sum(b, j):
        for way in both:
            h = first(way)
            s1_opposite(b, way, j).wait_recv()
            mine = chunk(b, h, way % 4, j)
            mine[...] = (mine[...].astype(F32) + (TB if b else TA)[j, h].astype(F32)).astype(BF)
            go(s1_summed(b, way, j))
        if j == 0:
            for way in both:
                go(s1_direct(b, way, 1))

    def s1_total(b, j):
        for way in both:
            s1_direct(b, way, j).wait_recv()
        for way in both:
            s1_summed(b, way, j).wait_recv()
        came = RB if b else RA
        for h in range(2):
            total = chunk(b, h, 0, j)[...].astype(F32) + came[j, 1 - h].astype(F32) + came[j, 2 + h].astype(F32)
            (QB if b else QA)[j, h] = total.astype(BF)
        for d in (2, 1, 3):
            go(s2(b, d, j))

    def s2(b, d, j):
        if b:
            src, dst, where = QB.at[j, :, d], R2B.at[d - 1, j], at(dy=d)
        else:
            src, dst, where = QA.at[j, :, x_hi(d), d % 2], R2A.at[d - 1, j], at(dx=d)
        return remote(src, dst, s2send, s2recv, b * 6 + j * 3 + d - 1, where)

    def s2_total(b, j):
        for d in (1, 3, 2):
            s2(b, d, j).wait_recv()
        if b:
            total, came = QB[j, :, 0].astype(F32), R2B
        else:
            total, came = QA[j, :, xh, 0].astype(F32), R2A
        for i in range(3):
            total = total + came[i, j].astype(F32)
        for h in range(2):
            for k in range(2):
                F[b * 4 + h * 2 + jz(j), k] = total[h, :, k * 128 : (k + 1) * 128].astype(BF)

    def s3(dz, dc):
        k = dz * 2 + dc
        return remote(
            F.at[(z + dz) % 8, (c + dc) % 2], R3.at[k], s3send, s3recv, k, at(dz=dz, dc=dc)
        )

    for j in range(2):
        for b in range(2):
            dx_part(b, j)
            for way in both:
                go(s1_opposite(b, way, j))
            if j == 1:
                for way in both:
                    go(s1_direct(b, way, 0))
    TT[0] = gate_term.T.astype(BF)
    TT[1] = up_term.T.astype(BF)
    grads_over_z(2, 1)
    grads(0, 0)
    grads(0, 1)
    grads(1, 2)
    s1_sum(0, 0)
    s1_sum(1, 0)
    grads_over_z(0)
    grads(1, 0)
    s1_sum(0, 1)
    s1_sum(1, 1)
    grads_over_z(1)
    grads(1, 1)
    for j in range(2):
        for b in range(2):
            s1_total(b, j)

    for m in (2, 0, 1):
        grad_to_sibling(1, m).wait_recv()
        outs[m][...] += RECV[1, m].astype(F32)

    told(3)
    before = len(sends)
    for j in range(2):
        for b in range(2):
            s2_total(b, j)
        for dz in (4, 3, 5, 2, 6, 1, 7, 0):
            for dc in range(2):
                if dz % 2 == j and (dz or dc):
                    go(s3(dz, dc))
    for copy in sends[:before]:
        copy.wait_send()

    def finish(m):
        for way in both:
            for h in (0, 1) if m == 2 else (None,):
                grad_over_z(m, way, h).wait_recv()
        done = 0
        if m == 2:
            for way in both:
                for other in (1, 0):
                    early_over_z(way, other).wait_recv()
            come = EARLYR[0].astype(F32) + EARLYR[1].astype(F32)
            outs[m][:, :EARLY] = (outs[m][:, :EARLY] + come) * (1.0 / 32.0)
            done = EARLY
        outs[m][:, done:] = (outs[m][:, done:] + ZRECV[m, :, done:].astype(F32)) * (1.0 / 32.0)

    finish(2)
    finish(0)
    finish(1)
    for dz in range(8):
        for dc in range(2):
            if dz or dc:
                s3(dz, dc).wait_recv()
    for odd in range(2):
        for dc in range(2):
            total = None
            for dz in range(odd, 8, 2):
                if dz == 0 and dc == 0:
                    term = F[z, c].astype(F32)
                else:
                    term = R3[dz * 2 + dc].astype(F32)
                total = term if total is None else total + term
            row = pl.multiple_of(((z + odd) % 2) * 64 + ((c + dc) % 2) * 32, 32)
            o_dx[pl.ds(row, 32), :] = total.astype(BF)
    for copy in sends[before:]:
        copy.wait_send()


def write_out(dx, g, u, d, o_dx, o_g, o_u, o_d, sem):
    copies = [
        pltpu.make_async_copy(src, dst, sem.at[k])
        for k, (src, dst) in enumerate(((g, o_g), (u, o_u), (d, o_d), (dx, o_dx)))
    ]
    for copy in copies:
        copy.start()
    for copy in copies:
        copy.wait()


def body(tokens, cotangent, step_lengths, step_labels, gate_weight, up_weight, down_weight):
    dma = pltpu.SemaphoreType.DMA
    hbm = pl.BlockSpec(memory_space=pltpu.HBM)
    smem = pl.BlockSpec(memory_space=pltpu.SMEM)
    vmem = pl.BlockSpec(memory_space=pltpu.VMEM)
    shapes = [((128, 128), BF)] + [((64, D), F32)] * 3
    held = pl.pallas_call(
        kernel,
        name="ffn_backward",
        out_shape=tuple(pltpu.VMEM(shape, dtype) for shape, dtype in shapes),
        in_specs=[smem, smem] + [hbm] * 5,
        out_specs=[vmem] * 4,
        scratch_shapes=[
            pltpu.VMEM((8, 2, 16, D), BF),
            pltpu.VMEM((8, 2, 16, D), BF),
            pltpu.VMEM((32, D), BF),
            pltpu.VMEM((3, 256, D), BF),
            pltpu.VMEM((3, 256, 256), F32),
            pltpu.VMEM((256, 512), BF),
            pltpu.VMEM((3, 256, 256), BF),
            pltpu.VMEM((2, 3, 64, D), BF),
            pltpu.VMEM((3, 64, D), F32),
            pltpu.VMEM((2, 3, 64, D), BF),
            pltpu.VMEM((3, 64, D), BF),
            pltpu.VMEM((3, 64, D), BF),
            pltpu.VMEM((128, EARLY), BF),
            pltpu.VMEM((2, 64, EARLY), BF),
            pltpu.VMEM((8, 2, 4, 2, 32, 256), BF),
            pltpu.VMEM((2, 2, 2, 2, 32, 256), BF),
            pltpu.VMEM((2, 2, 4, 32, 256), BF),
            pltpu.VMEM((2, 4, 2, 2, 32, 256), BF),
            pltpu.VMEM((2, 4, 4, 32, 256), BF),
            pltpu.VMEM((2, 2, 2, 2, 32, 256), BF),
            pltpu.VMEM((2, 2, 4, 32, 256), BF),
            pltpu.VMEM((3, 2, 2, 32, 256), BF),
            pltpu.VMEM((3, 2, 2, 32, 256), BF),
            pltpu.VMEM((8, 2, 32, 128), BF),
            pltpu.VMEM((16, 32, 128), BF),
            dma((6,)), dma((22,)), dma((22,)), dma((24,)), dma((24,)),
            dma((6,)), dma((6,)), dma((6,)), dma((6,)),
            dma((7,)), dma((7,)), dma((8,)), dma((8,)),
            dma((24,)), dma((24,)), dma((12,)), dma((12,)), dma((16,)), dma((16,)),
            dma((4,)), dma((4,)), pltpu.SemaphoreType.REGULAR((4,)),
        ],
        compiler_params=pltpu.CompilerParams(
            collective_id=0, has_side_effects=True, vmem_limit_bytes=60 * 2**20 + 2**19
        ),
        cost_estimate=pl.CostEstimate(flops=4_300_000_000, bytes_accessed=8_000_000, transcendentals=65536),
    )(step_lengths, step_labels, tokens, cotangent, gate_weight, up_weight, down_weight)
    return pl.pallas_call(
        write_out,
        name="write_out",
        out_shape=tuple(jax.ShapeDtypeStruct(shape, dtype) for shape, dtype in shapes),
        in_specs=[vmem] * 4,
        out_specs=[hbm] * 4,
        scratch_shapes=[dma((4,))],
        compiler_params=pltpu.CompilerParams(vmem_limit_bytes=2**20),
    )(*held)


def solution(mesh):
    return jax.shard_map(
        body,
        mesh=mesh,
        in_specs=(
            P("weight", None),
            P("weight", None),
            P("weight", None),
            P("weight", None),
            P(("dp", "weight"), None),
            P(("dp", "weight"), None),
            P(("dp", "weight"), None),
        ),
        out_specs=(
            P("weight", "dp"),
            P(("dp", "weight"), None),
            P(("dp", "weight"), None),
            P(("dp", "weight"), None),
        ),
        check_vma=False,
    )
```

```python
import jax
import jax.numpy as jnp
from jax import lax
from jax.experimental import pallas as pl
from jax.experimental.pallas import tpu as pltpu
from jax.sharding import PartitionSpec as P

MESH = pl.DeviceIdType.MESH
BF = jnp.bfloat16
F32 = jnp.float32
D = 4096
HALF = D // 2
EARLY = 1024
ROWS = 128


def nt(left, right):
    return lax.dot_general(left, right, (((1,), (1,)), ((), ())), preferred_element_type=F32)


def nn(left, right):
    return jnp.dot(left, right, preferred_element_type=F32)


def kernel(
    lens_in, labs_in, tok, cot, wg, wu, wd,
    o_dx, o_g, o_u, o_d,
    lens, labs, X, C, CT, W, ACC, TERMS, TT, SEND, OWNZ, RECV, ZSEND, ZRECV, EARLYS, EARLYR,
    PART, TA, TB, RA, RB, QA, QB, R2A, R2B, F, R3,
    in_sem, ysend, yrecv, xsend, xrecv, zsend, zrecv, dsend, drecv,
    gsend, grecv, zgsend, zgrecv, s1send, s1recv, s2send, s2recv, s3send, s3recv, esend, erecv, there,
):
    dp = lax.axis_index("dp")
    wt = lax.axis_index("weight")
    z, xh, c = dp // 4, (dp // 2) % 2, dp % 2
    y, xl = wt // 2, wt % 2
    x = xh * 2 + xl

    def at(dx=0, dy=0, dz=0, dc=0):
        xx = (x + dx) % 4
        yy = (y + dy) % 4
        zz = (z + dz) % 8
        cc = (c + dc) % 2
        return (zz * 4 + (xx // 2) * 2 + cc, yy * 2 + xx % 2)

    def remote(src, dst, ssem, rsem, k, where):
        return pltpu.make_async_remote_copy(
            src_ref=src, dst_ref=dst, send_sem=ssem.at[k], recv_sem=rsem.at[k],
            device_id=where, device_id_type=MESH,
        )

    sends = []

    def go(copy):
        copy.start()
        sends.append(copy)
        return copy

    barrier = pltpu.get_barrier_semaphore()
    column = [at(dc=1), at(dz=1), at(dz=-1)]
    partners = column + [at(dy=1), at(dy=-1), at(dx=1), at(dx=-1)]
    for who in partners:
        pl.semaphore_signal(barrier, inc=1, device_id=who, device_id_type=MESH)

    def tell(r):
        for who in column:
            pl.semaphore_signal(there.at[r], inc=1, device_id=who, device_id_type=MESH)

    def told(r):
        pl.semaphore_wait(there.at[r], len(column))

    row0 = pl.multiple_of((z % 2) * 64 + c * 32, 32)
    loads = [pltpu.make_async_copy(cot.at[pl.ds(row0, 32)], CT, in_sem.at[0])]
    for p in range(2):
        loads.append(pltpu.make_async_copy(tok.at[pl.ds(row0 + 16 * p, 16)], X.at[0, p], in_sem.at[1 + p]))
    for m, ref in enumerate((wg, wu, wd)):
        loads.append(pltpu.make_async_copy(ref, W.at[m, pl.ds(192, 64)], in_sem.at[3 + m]))
    steps = [
        pltpu.make_async_copy(lens_in, lens, in_sem.at[6]),
        pltpu.make_async_copy(labs_in, labs, in_sem.at[7]),
    ]
    for copy in loads + steps:
        copy.start()

    for copy in loads[1:]:
        copy.wait()
    pl.semaphore_wait(barrier, len(partners))

    def first(way):
        return 0 if way == 1 else 1

    def side(way):
        return 3 if way == 1 else 1

    def part(a, slot, p):
        return C.at[slot, p, :, pl.ds((a - 1) * HALF, HALF)] if a else X.at[slot, p]

    def y_piece(a, p, way):
        k = first(way) * 11 + a * 2 + p
        return remote(part(a, 0, p), part(a, side(way) * 2, p), ysend, yrecv, k, at(dy=way))

    def y_next(a, way):
        p = first(way)
        k = first(way) * 11 + 6 + a
        return remote(part(a, side(way) * 2, p), part(a, 4, p), ysend, yrecv, k, at(dy=way))

    def y_other(a, way):
        p = first(way)
        k = first(way) * 11 + 8 + a
        return remote(part(a, side(way) * 2 + 1, p), part(a, 5, p), ysend, yrecv, k, at(dy=way))

    def x_piece(a, p, dy):
        k = p * 12 + dy * 3 + a
        return remote(
            part(a, dy * 2, p), part(a, dy * 2 + 1, p), xsend, xrecv, k, at(dx=1 if p == 0 else -1)
        )

    def z_weights(m, way):
        rows = (192, 64) if way == 1 else (224, 96)
        return remote(
            W.at[m, pl.ds(rows[0], 32)], W.at[m, pl.ds(rows[1], 32)],
            zsend, zrecv, m * 2 + first(way), at(dz=way),
        )

    def d_own(m):
        return remote(W.at[m, pl.ds(192, 64)], W.at[m, pl.ds(128, 64)], dsend, drecv, m, at(dc=1))

    def d_forward(m):
        return remote(W.at[m, pl.ds(64, 64)], W.at[m, pl.ds(0, 64)], dsend, drecv, 3 + m, at(dc=1))

    both = (1, -1)

    def weights_on(m):
        for way in both:
            z_weights(m, way).wait_recv()
        go(d_forward(m))

    for way in both:
        go(y_piece(0, first(way), way))
    for p in range(2):
        go(x_piece(0, p, 0))
    for m in range(3):
        for way in both:
            go(z_weights(m, way))
        if m == 0:
            for way in both:
                go(y_piece(0, 1 - first(way), way))
    for m in range(3):
        go(d_own(m))
    tell(0)

    for copy in steps:
        copy.wait()
    position = lax.broadcasted_iota(jnp.int32, (32, 128), 0) + row0
    segment = jnp.zeros((32, 128), jnp.int32)
    end = lens[0, 0]
    segment = segment + (position >= end).astype(jnp.int32)
    for k in range(1, 4):
        end = end + lens[0, k]
        segment = segment + (position >= end).astype(jnp.int32)
    length = jnp.zeros((32, 128), jnp.int32)
    label = jnp.zeros((32, 128), jnp.int32)
    for k in range(4):
        length = jnp.where(segment == k, lens[0, k], length)
        label = jnp.where(segment == k, labs[0, k], label)
    factor = (1.0 + 2.0 * label.astype(F32)) * lax.rsqrt(length.astype(F32) * 4 / ROWS)
    loads[0].wait()
    for j in range(D // 128):
        cols = slice(j * 128, (j + 1) * 128)
        value = (CT[:, cols].astype(F32) * factor).astype(BF)
        C[0, 0, :, cols] = value[:16]
        C[0, 1, :, cols] = value[16:]
    for a in (1, 2):
        for p in range(2):
            go(x_piece(a, p, 0))
        for way in both:
            go(y_piece(a, first(way), way))
    for way in both:
        y_piece(0, first(way), way).wait_recv()
        go(y_next(0, way))
        go(x_piece(0, first(way), side(way)))
    for a in (1, 2):
        for way in both:
            go(y_piece(a, 1 - first(way), way))
    for way in both:
        y_piece(0, 1 - first(way), way).wait_recv()
        go(x_piece(0, 1 - first(way), side(way)))
    weights_on(0)
    told(0)
    tell(1)
    for a in (1, 2):
        for way in both:
            y_piece(a, first(way), way).wait_recv()
            go(x_piece(a, first(way), side(way)))
            go(y_next(a, way))
    for way in both:
        y_next(0, way).wait_recv()
        go(x_piece(0, first(way), 2))
    weights_on(1)
    told(1)
    tell(2)
    for a in (1, 2):
        for way in both:
            y_piece(a, 1 - first(way), way).wait_recv()
            go(x_piece(a, 1 - first(way), side(way)))
        for way in both:
            x_piece(a, first(way), side(way)).wait_recv()
            go(y_other(a, way))
    weights_on(2)
    told(2)
    tell(3)

    def contract(m, ref):
        ACC[m] = nt(ref[...].reshape(256, D), W[m])

    for m in range(2):
        d_own(m).wait_recv()
        d_forward(m).wait_recv()
    for dy in (0, 3, 1, 2):
        for p in range(2):
            x_piece(0, p, dy).wait_recv()
    contract(0, X)
    contract(1, X)
    gate, up = ACC[0], ACC[1]
    sig = jax.nn.sigmoid(gate)
    act = gate * sig
    TT[2] = (act * up).T.astype(BF)

    def weighted_here(a):
        for way in both:
            y_next(a, way).wait_recv()
        for way in both:
            x_piece(a, 1 - first(way), side(way)).wait_recv()
        for p in range(2):
            x_piece(a, p, 0).wait_recv()
        for way in both:
            y_other(a, way).wait_recv()

    outs = (o_g, o_u, o_d)

    def block_of(ref, h):
        if h is None:
            return ref
        return ref.at[:, EARLY:HALF] if h == 0 else ref.at[:, HALF:]

    def grad_to_sibling(half, m, h=None):
        k = half * 3 + m if h != 1 else 6
        return remote(
            block_of(SEND.at[half, m], h), block_of(RECV.at[half, m], h), gsend, grecv, k, at(dc=1)
        )

    def early_over_z(way, other):
        row = 0 if way == -1 else 32
        return remote(
            EARLYS.at[pl.ds((64 if other == 0 else 0) + row, 32)], EARLYR.at[other, pl.ds(row, 32)],
            esend, erecv, first(way) * 2 + other, at(dz=way, dc=other),
        )

    def grads(half, m, h=None):
        if m == 2:
            right = C[...] if h is None else C[:, :, :, h * HALF : (h + 1) * HALF]
        else:
            right = X[...]
        value = nn(TT[m, pl.ds(half * 128, 128)], right.reshape(256, right.shape[-1]))
        if h == 0:
            EARLYS[...] = value[:, :EARLY].astype(BF)
            for way in both:
                for other in (1, 0):
                    go(early_over_z(way, other))
            value = value[:, EARLY:]
        block_of(SEND.at[half, m], h)[...] = value[:64].astype(BF)
        block_of(outs[m] if half else OWNZ.at[m], h)[...] = value[64:]
        go(grad_to_sibling(half, m, h))

    def grad_over_z(m, way, h=None):
        rows = pl.ds(0 if way == -1 else 32, 32)
        k = (m if h != 1 else 3) * 2 + first(way)
        return remote(
            block_of(ZSEND.at[m, rows], h), block_of(ZRECV.at[m, rows], h), zgsend, zgrecv, k, at(dz=way)
        )

    def grads_over_z(m, h=None):
        grad_to_sibling(0, m, h).wait_recv()
        mine, came = block_of(OWNZ.at[m], h), block_of(RECV.at[0, m], h)
        block_of(ZSEND.at[m], h)[...] = (mine[...] + came[...].astype(F32)).astype(BF)
        for way in both:
            go(grad_over_z(m, way, h))

    weighted_here(1)
    grads(0, 2, 0)
    weighted_here(2)
    d_own(2).wait_recv()
    d_forward(2).wait_recv()
    contract(2, C)
    grads(0, 2, 1)
    grads_over_z(2, 0)
    hidden_grad = ACC[2]
    gate, up = ACC[0], ACC[1]
    sig = jax.nn.sigmoid(gate)
    act = gate * sig
    gate_term = hidden_grad * up * sig * (1.0 + gate * (1.0 - sig))
    up_term = hidden_grad * act
    TERMS[:, :256] = gate_term.astype(BF)
    TERMS[:, 256:] = up_term.astype(BF)

    def dx_part(b, j):
        for h in range(2):
            place = b * 4 + h * 2 + jz(j)
            cols = pl.ds(pl.multiple_of(place * 512, 512), 512)
            value = nn(TERMS[...], W[0:2, :, cols].reshape(512, 512)).astype(BF)
            for k in range(2):
                PART[place, k] = value[:, k * 256 : (k + 1) * 256].reshape(4, 2, 32, 256)

    def x_hi(dx):
        return ((x + dx) % 4) // 2

    def jz(j):
        return (z + j) % 2

    def chunk(b, h, to, j):
        if b:
            return PART.at[4 + h * 2 + jz(j), x_hi(to), :, to % 2]
        return PART.at[h * 2 + jz(j), :, to]

    def along(b, way):
        return at(dx=way) if b else at(dy=way)

    def s1_opposite(b, way, j):
        h = first(way)
        return remote(chunk(b, h, 2, j), (TB if b else TA).at[j, h], s1send, s1recv, b * 12 + j * 6 + h, along(b, way))

    def s1_direct(b, way, j):
        i = first(way)
        return remote(
            chunk(b, 1 - i, way % 4, j), (RB if b else RA).at[j, i],
            s1send, s1recv, b * 12 + j * 6 + 2 + i, along(b, way),
        )

    def s1_summed(b, way, j):
        i = first(way)
        return remote(
            chunk(b, i, way % 4, j), (RB if b else RA).at[j, 2 + i],
            s1send, s1recv, b * 12 + j * 6 + 4 + i, along(b, way),
        )

    def s1_sum(b, j):
        for way in both:
            h = first(way)
            s1_opposite(b, way, j).wait_recv()
            mine = chunk(b, h, way % 4, j)
            mine[...] = (mine[...].astype(F32) + (TB if b else TA)[j, h].astype(F32)).astype(BF)
            go(s1_summed(b, way, j))
        if j == 0:
            for way in both:
                go(s1_direct(b, way, 1))

    def s1_total(b, j):
        for way in both:
            s1_direct(b, way, j).wait_recv()
        for way in both:
            s1_summed(b, way, j).wait_recv()
        came = RB if b else RA
        for h in range(2):
            total = chunk(b, h, 0, j)[...].astype(F32) + came[j, 1 - h].astype(F32) + came[j, 2 + h].astype(F32)
            (QB if b else QA)[j, h] = total.astype(BF)
        for d in (2, 1, 3):
            go(s2(b, d, j))

    def s2(b, d, j):
        if b:
            src, dst, where = QB.at[j, :, d], R2B.at[d - 1, j], at(dy=d)
        else:
            src, dst, where = QA.at[j, :, x_hi(d), d % 2], R2A.at[d - 1, j], at(dx=d)
        return remote(src, dst, s2send, s2recv, b * 6 + j * 3 + d - 1, where)

    def s2_total(b, j):
        for d in (1, 3, 2):
            s2(b, d, j).wait_recv()
        if b:
            total, came = QB[j, :, 0].astype(F32), R2B
        else:
            total, came = QA[j, :, xh, 0].astype(F32), R2A
        for i in range(3):
            total = total + came[i, j].astype(F32)
        for h in range(2):
            for k in range(2):
                F[b * 4 + h * 2 + jz(j), k] = total[h, :, k * 128 : (k + 1) * 128].astype(BF)

    def s3(dz, dc):
        k = dz * 2 + dc
        return remote(
            F.at[(z + dz) % 8, (c + dc) % 2], R3.at[k], s3send, s3recv, k, at(dz=dz, dc=dc)
        )

    for j in range(2):
        for b in range(2):
            dx_part(b, j)
            for way in both:
                go(s1_opposite(b, way, j))
            if j == 1:
                for way in both:
                    go(s1_direct(b, way, 0))
    TT[0] = gate_term.T.astype(BF)
    TT[1] = up_term.T.astype(BF)
    grads_over_z(2, 1)
    grads(0, 0)
    grads(0, 1)
    grads(1, 2)
    s1_sum(0, 0)
    s1_sum(1, 0)
    grads_over_z(0)
    grads(1, 0)
    s1_sum(0, 1)
    s1_sum(1, 1)
    grads_over_z(1)
    grads(1, 1)
    for j in range(2):
        for b in range(2):
            s1_total(b, j)

    for m in (2, 0, 1):
        grad_to_sibling(1, m).wait_recv()
        outs[m][...] += RECV[1, m].astype(F32)

    told(3)
    before = len(sends)
    for j in range(2):
        for b in range(2):
            s2_total(b, j)
        for dz in (4, 3, 5, 2, 6, 1, 7, 0):
            for dc in range(2):
                if dz % 2 == j and (dz or dc):
                    go(s3(dz, dc))
    for copy in sends[:before]:
        copy.wait_send()

    def finish(m):
        for way in both:
            for h in (0, 1) if m == 2 else (None,):
                grad_over_z(m, way, h).wait_recv()
        done = 0
        if m == 2:
            for way in both:
                for other in (1, 0):
                    early_over_z(way, other).wait_recv()
            come = EARLYR[0].astype(F32) + EARLYR[1].astype(F32)
            outs[m][:, :EARLY] = (outs[m][:, :EARLY] + come) * (1.0 / 32.0)
            done = EARLY
        outs[m][:, done:] = (outs[m][:, done:] + ZRECV[m, :, done:].astype(F32)) * (1.0 / 32.0)

    finish(2)
    finish(0)
    finish(1)
    for dz in range(8):
        for dc in range(2):
            if dz or dc:
                s3(dz, dc).wait_recv()
    for odd in range(2):
        for dc in range(2):
            total = None
            for dz in range(odd, 8, 2):
                if dz == 0 and dc == 0:
                    term = F[z, c].astype(F32)
                else:
                    term = R3[dz * 2 + dc].astype(F32)
                total = term if total is None else total + term
            row = pl.multiple_of(((z + odd) % 2) * 64 + ((c + dc) % 2) * 32, 32)
            o_dx[pl.ds(row, 32), :] = total.astype(BF)
    for copy in sends[before:]:
        copy.wait_send()


def write_out(dx, g, u, d, o_dx, o_g, o_u, o_d, sem):
    copies = [
        pltpu.make_async_copy(src, dst, sem.at[k])
        for k, (src, dst) in enumerate(((g, o_g), (u, o_u), (d, o_d), (dx, o_dx)))
    ]
    for copy in copies:
        copy.start()
    for copy in copies:
        copy.wait()


def body(tokens, cotangent, step_lengths, step_labels, gate_weight, up_weight, down_weight):
    dma = pltpu.SemaphoreType.DMA
    hbm = pl.BlockSpec(memory_space=pltpu.HBM)
    vmem = pl.BlockSpec(memory_space=pltpu.VMEM)
    shapes = [((128, 128), BF)] + [((64, D), F32)] * 3
    held = pl.pallas_call(
        kernel,
        name="ffn_backward",
        out_shape=tuple(pltpu.VMEM(shape, dtype) for shape, dtype in shapes),
        in_specs=[hbm] * 7,
        out_specs=[vmem] * 4,
        scratch_shapes=[
            pltpu.SMEM((1, 4), jnp.int32),
            pltpu.SMEM((1, 4), jnp.int32),
            pltpu.VMEM((8, 2, 16, D), BF),
            pltpu.VMEM((8, 2, 16, D), BF),
            pltpu.VMEM((32, D), BF),
            pltpu.VMEM((3, 256, D), BF),
            pltpu.VMEM((3, 256, 256), F32),
            pltpu.VMEM((256, 512), BF),
            pltpu.VMEM((3, 256, 256), BF),
            pltpu.VMEM((2, 3, 64, D), BF),
            pltpu.VMEM((3, 64, D), F32),
            pltpu.VMEM((2, 3, 64, D), BF),
            pltpu.VMEM((3, 64, D), BF),
            pltpu.VMEM((3, 64, D), BF),
            pltpu.VMEM((128, EARLY), BF),
            pltpu.VMEM((2, 64, EARLY), BF),
            pltpu.VMEM((8, 2, 4, 2, 32, 256), BF),
            pltpu.VMEM((2, 2, 2, 2, 32, 256), BF),
            pltpu.VMEM((2, 2, 4, 32, 256), BF),
            pltpu.VMEM((2, 4, 2, 2, 32, 256), BF),
            pltpu.VMEM((2, 4, 4, 32, 256), BF),
            pltpu.VMEM((2, 2, 2, 2, 32, 256), BF),
            pltpu.VMEM((2, 2, 4, 32, 256), BF),
            pltpu.VMEM((3, 2, 2, 32, 256), BF),
            pltpu.VMEM((3, 2, 2, 32, 256), BF),
            pltpu.VMEM((8, 2, 32, 128), BF),
            pltpu.VMEM((16, 32, 128), BF),
            dma((8,)), dma((22,)), dma((22,)), dma((24,)), dma((24,)),
            dma((6,)), dma((6,)), dma((6,)), dma((6,)),
            dma((7,)), dma((7,)), dma((8,)), dma((8,)),
            dma((24,)), dma((24,)), dma((12,)), dma((12,)), dma((16,)), dma((16,)),
            dma((4,)), dma((4,)), pltpu.SemaphoreType.REGULAR((4,)),
        ],
        compiler_params=pltpu.CompilerParams(
            collective_id=0, has_side_effects=True, vmem_limit_bytes=60 * 2**20 + 2**19
        ),
        cost_estimate=pl.CostEstimate(flops=4_300_000_000, bytes_accessed=8_000_000, transcendentals=65536),
    )(step_lengths, step_labels, tokens, cotangent, gate_weight, up_weight, down_weight)
    return pl.pallas_call(
        write_out,
        name="write_out",
        out_shape=tuple(jax.ShapeDtypeStruct(shape, dtype) for shape, dtype in shapes),
        in_specs=[vmem] * 4,
        out_specs=[hbm] * 4,
        scratch_shapes=[dma((4,))],
        compiler_params=pltpu.CompilerParams(vmem_limit_bytes=2**20),
    )(*held)


def solution(mesh):
    return jax.shard_map(
        body,
        mesh=mesh,
        in_specs=(
            P("weight", None),
            P("weight", None),
            P("weight", None),
            P("weight", None),
            P(("dp", "weight"), None),
            P(("dp", "weight"), None),
            P(("dp", "weight"), None),
        ),
        out_specs=(
            P("weight", "dp"),
            P(("dp", "weight"), None),
            P(("dp", "weight"), None),
            P(("dp", "weight"), None),
        ),
        check_vma=False,
    )
```
